512 devices in a mesh: ctx: 64 (over x, y, core), tp: 8 (over z).
Axes of the slice: x: 4, y: 8, z: 8, core: 2. Of those that a mesh axis runs over, the one named last changes fastest.
Arguments:
- queries: bfloat16 [8, 64, 8192], P(None, 'ctx', 'tp'), may hold values from -16 to 16
- node_kv: bfloat16 [8, 64, 2048], P(None, 'ctx', 'tp'), may hold values from -6 to 6
- key_value_pool: bfloat16 [4608, 64, 2048], P('ctx', None, 'tp'), may hold values from -6 to 6
- out_weight: bfloat16 [8192, 8192], P('tp', 'ctx'), may hold values from -0.0625 to 0.0625
- parents: int32 [8, 64], replicated, may hold values from -1 to 62, as said below
- accepted_path: int32 [8, 8], replicated, may hold values from 0 to 62, as said below
- accept_count: int32 [8], replicated, may hold values from 1 to 8
- lengths: int32 [8], replicated, may hold values from 4096 to 32760, as said below
- page_table: int32 [8, 512], P(None, 'ctx'), may hold values from 0 to 71, as said below
- free_slot: int32 [8, 64], P(None, 'ctx'), may hold values from 0 to 71, as said below
Outputs:
- projected: float32 [8, 64, 8192], P(None, 'tp', 'ctx')
- updated_pool: bfloat16 [4608, 64, 2048], P('ctx', None, 'tp')
- new_page_table: int32 [8, 512], P(None, 'ctx')
The draws below stay inside these ranges and needn't reach their ends.
Inputs may be any that keep to these rules, and one draw needn't show every extreme that they name: parents[r, 0] = -1, and every other node's parent has a smaller index than the node. accepted_path[r, 0] = 0 and accepted_path[r, j] is the parent of accepted_path[r, j + 1]. Requests 2k and 2k + 1 that share pages have equal lengths. page_table[r, p] is a slot of the pool of ctx index p div 8. Entries are distinct except that request 2k + 1 may share its pages 0 to lengths[2k] div 64 with request 2k; no page after a request's tail page is shared. free_slot[r, c] is a slot of ctx index c that no entry of page_table names; distinct over r.
All inputs are finite; a program needn't handle non-finite values.
Results may differ from the reference program's by a relative error of at most 0.0027.
Values may be sent and summed in bfloat16 or wider, within the bound.
No kernel may reach another device: no remote copies, remote signals or barrier semaphores. Data moves between devices by JAX's collectives and lax.ppermute only.
A program may use at most 64 MiB of HBM per device.

```python
import jax
import jax.numpy as jnp
from jax import lax

QUERY_HEADS = 64
KEY_VALUE_HEADS = 8
HEAD_WIDTH = 128
D = 8192
TREE_NODES = 64
PATH_ROWS = 8
PAGE_ROWS = 64
REQUEST_COUNT = 8
PPD = 8
CACHE_LENGTH = 32768
PAGES = 512
POOL_DEV = 72
POOL_SLOTS = 4608
N_CTX = 64


def tree_shape(base_key):
    folded = jax.random.fold_in(base_key, 11)
    subkeys = jax.random.split(folded, 2)
    node_ids = jnp.arange(TREE_NODES, dtype=jnp.int32)
    upper_bound = jnp.maximum(node_ids, 1)
    drawn = jax.random.randint(subkeys[0], (REQUEST_COUNT, TREE_NODES), 0, upper_bound[None, :])
    candidates = jnp.tile(jnp.arange(1, TREE_NODES - 1, dtype=jnp.int32)[None, :], (REQUEST_COUNT, 1))
    shuffled = jax.random.permutation(subkeys[1], candidates, axis=1, independent=True)
    chosen = jnp.sort(shuffled[:, :PATH_ROWS - 1], axis=1)
    chosen = chosen.at[0, PATH_ROWS - 2].set(TREE_NODES - 2)
    chain = jnp.concatenate([jnp.zeros((REQUEST_COUNT, 1), jnp.int32), chosen], axis=1).astype(jnp.int32)
    request_ids = jnp.arange(REQUEST_COUNT, dtype=jnp.int32)[:, None]
    parents = drawn.at[request_ids, chain[:, 1:]].set(chain[:, :-1])
    parents = parents.at[:, TREE_NODES - 1].set(TREE_NODES - 2)
    parents = parents.at[:, 0].set(-1)
    return (parents.astype(jnp.int32), chain)


def draw_parents(key, part):
    return tree_shape(key)[0]


def draw_accepted_path(key, part):
    return tree_shape(key)[1]


def draw_accept_count(key, part):
    subkeys = jax.random.split(jax.random.fold_in(key, 23), 2)
    counts = jax.random.randint(subkeys[0], (REQUEST_COUNT,), 1, PATH_ROWS + 1)
    ordering = jax.random.permutation(subkeys[1], REQUEST_COUNT)
    return counts.at[ordering[0]].set(PATH_ROWS).at[ordering[1]].set(1).astype(jnp.int32)


def context_layout(base_key):
    folded = jax.random.fold_in(base_key, 37)
    subkeys = jax.random.split(folded, 5)
    pair_count = REQUEST_COUNT // 2
    top_pair = jax.random.randint(subkeys[0], (), 0, pair_count)
    low_pair = (top_pair + 1 + jax.random.randint(subkeys[1], (), 0, pair_count - 1)) % pair_count
    lengths = jax.random.randint(subkeys[2], (REQUEST_COUNT,), CACHE_LENGTH // 8, CACHE_LENGTH - PATH_ROWS + 1)
    lengths = lengths.at[2 * top_pair].set(CACHE_LENGTH - PATH_ROWS).at[2 * low_pair + 1].set(CACHE_LENGTH // 8)
    forked = jax.random.randint(subkeys[3], (pair_count,), 0, 2)
    forked = forked.at[top_pair].set(1).at[low_pair].set(0)
    even_len = lengths[0::2]
    lengths = lengths.at[1::2].set(jnp.where(forked == 1, even_len, lengths[1::2]))
    slot_perm = jax.random.permutation(subkeys[4], jnp.tile(jnp.arange(POOL_DEV, dtype=jnp.int32)[None, :], (N_CTX, 1)), axis=1, independent=True)
    owned = slot_perm[:, :REQUEST_COUNT * PPD].reshape(N_CTX, REQUEST_COUNT, PPD)
    slot_table = owned.transpose(1, 0, 2).reshape(REQUEST_COUNT, PAGES)
    spare_slots = slot_perm[:, REQUEST_COUNT * PPD:].transpose(1, 0)
    tail_page = even_len // PAGE_ROWS
    page_ids = jnp.arange(PAGES, dtype=jnp.int32)
    shared = (forked[:, None] == 1) & (page_ids[None, :] <= tail_page[:, None])
    slot_table = slot_table.at[1::2].set(jnp.where(shared, slot_table[0::2], slot_table[1::2]))
    return (lengths.astype(jnp.int32), slot_table.astype(jnp.int32), spare_slots.astype(jnp.int32))


def draw_lengths(key, part):
    return context_layout(key)[0]


def draw_page_table(key, part):
    return context_layout(key)[1]


def draw_free_slot(key, part):
    return context_layout(key)[2]


def aligned_parts(base_key):
    folded = jax.random.fold_in(base_key, 51)
    subkeys = jax.random.split(folded, 2)
    sign_vector = jnp.where(jax.random.bernoulli(subkeys[0], 0.5, (HEAD_WIDTH,)), 1.0, -1.0).astype(jnp.float32)
    strength = jax.random.uniform(subkeys[1], (REQUEST_COUNT, QUERY_HEADS), jnp.float32, 32.0, 64.0) * HEAD_WIDTH ** (-0.5)
    return (sign_vector, strength)


def draw_queries(key, part):
    folded = jax.random.fold_in(key, 61)
    complete_shape = (REQUEST_COUNT, TREE_NODES, QUERY_HEADS, HEAD_WIDTH)
    value_rows = jnp.clip(3.0 * jax.random.normal(folded, complete_shape, jnp.float32), -16.0, 16.0)
    sign_vector, strength = aligned_parts(key)
    value_rows = value_rows.at[:, 1].set(strength[:, :, None] * sign_vector[None, None, :])
    return value_rows.reshape(REQUEST_COUNT, TREE_NODES, QUERY_HEADS * HEAD_WIDTH).astype(jnp.bfloat16)


def draw_node_kv(key, part):
    folded = jax.random.fold_in(key, 71)
    complete_shape = (REQUEST_COUNT, TREE_NODES, KEY_VALUE_HEADS, 2, HEAD_WIDTH)
    value_rows = jnp.clip(jax.random.normal(folded, complete_shape, jnp.float32), -6.0, 6.0)
    sign_vector, strength = aligned_parts(key)
    value_rows = value_rows.at[:, 0, :, 0].set(4.5 * sign_vector)
    value_rows = value_rows.at[:, 1, :, 0].set(4.46875 * sign_vector)
    return value_rows.reshape(REQUEST_COUNT, TREE_NODES, KEY_VALUE_HEADS * 2 * HEAD_WIDTH).astype(jnp.bfloat16)


def block_levels(key, dims, pieces, smallest, largest):
    def one(axis_at, blocks):
        heights = jax.random.uniform(jax.random.fold_in(jax.random.fold_in(key, 6), axis_at), (blocks,), jnp.float32, smallest / len(pieces), largest / len(pieces))
        return jnp.repeat(jnp.exp(heights), dims[axis_at] // blocks).reshape((-1,) + (1,) * (len(dims) - axis_at - 1))

    level = one(*pieces[0])
    for cut in pieces[1:]:
        level = level * one(*cut)
    return level


def gaussian(stream_key, extent, deviation, reach, cuts=(), kind=jnp.bfloat16):
    entries = deviation * jax.random.normal(stream_key, extent, jnp.float32)
    if cuts:
        entries = entries * block_levels(stream_key, extent, cuts, -0.22, 0.18)
    return jnp.clip(entries, -reach, reach).astype(kind)


def setup_inputs(seed: int = 0) -> dict:
    arg_keys = jax.random.split(jax.random.key(seed), 11)
    return {
        "queries": draw_queries(jax.random.fold_in(arg_keys[10], 71), 0),
        "node_kv": draw_node_kv(jax.random.fold_in(arg_keys[10], 71), 0),
        "key_value_pool": gaussian(arg_keys[2], (POOL_SLOTS, PAGE_ROWS, 2 * KEY_VALUE_HEADS * HEAD_WIDTH), 1.0, 6.0, ((0, 64), (2, 8))),
        "out_weight": gaussian(arg_keys[3], (QUERY_HEADS * HEAD_WIDTH, D), (QUERY_HEADS * HEAD_WIDTH) ** -0.5, 0.0625, ((0, 8), (1, 64))),
        "parents": draw_parents(jax.random.fold_in(arg_keys[10], 71), 0),
        "accepted_path": draw_accepted_path(jax.random.fold_in(arg_keys[10], 71), 0),
        "accept_count": draw_accept_count(jax.random.fold_in(arg_keys[10], 71), 0),
        "lengths": draw_lengths(jax.random.fold_in(arg_keys[10], 71), 0),
        "page_table": draw_page_table(jax.random.fold_in(arg_keys[10], 71), 0),
        "free_slot": draw_free_slot(jax.random.fold_in(arg_keys[10], 71), 0),
    }


masked_score = -1.0e30


def ancestry(parents):
    node_count = parents.shape[-1]
    node_ids = jnp.arange(node_count, dtype=jnp.int32)
    reached = (parents[:, :, None] == node_ids[None, None, :]).astype(jnp.float32)
    reached = reached + jnp.eye(node_count, dtype=jnp.float32)[None]
    for squaring in range(max(1, (node_count - 1).bit_length())):
        reached = jnp.minimum(jnp.einsum("rij,rjk->rik", reached, reached, precision=lax.Precision.HIGHEST), 1.0)
    return reached


def reference(queries, node_kv, key_value_pool, out_weight, parents, accepted_path, accept_count, lengths, page_table, free_slot):
    query_group_width = QUERY_HEADS // KEY_VALUE_HEADS
    score_scale = HEAD_WIDTH ** -0.5
    highest = lax.Precision.HIGHEST
    tree_mask = ancestry(parents)
    owner_ids = (jnp.arange(PAGES, dtype=jnp.int32) // PPD).astype(jnp.int32)
    global_table = (owner_ids[None, :] * POOL_DEV + page_table).astype(jnp.int32)
    positions = jnp.arange(CACHE_LENGTH, dtype=jnp.int32)

    def per_request(inputs):
        query_per_request, nodes_per_request, table_per_request, mask_r, length_r = inputs
        cache_per_request = key_value_pool[table_per_request].reshape(CACHE_LENGTH, KEY_VALUE_HEADS, 2, HEAD_WIDTH)
        cache_live = (positions < length_r)[None, None, :]
        tree_live = (mask_r > 0.5)[:, None, :]

        def per_head(head_inputs):
            query_h, cache_h, nodes_h = head_inputs
            query_f = query_h.astype(jnp.float32)
            cache_scores = jnp.einsum("ngd,td->ngt", query_f, cache_h[:, 0].astype(jnp.float32), precision=highest) * score_scale
            tree_scores = jnp.einsum("ngd,jd->ngj", query_f, nodes_h[:, 0].astype(jnp.float32), precision=highest) * score_scale
            row_max = jnp.maximum(
                jnp.max(jnp.where(cache_live, cache_scores, masked_score), axis=-1),
                jnp.max(jnp.where(tree_live, tree_scores, masked_score), axis=-1))
            cache_weights = jnp.where(cache_live, jnp.exp(jnp.where(cache_live, cache_scores, row_max[..., None]) - row_max[..., None]), 0.0)
            tree_weights = jnp.where(tree_live, jnp.exp(jnp.where(tree_live, tree_scores, row_max[..., None]) - row_max[..., None]), 0.0)
            row_sum = jnp.sum(cache_weights, axis=-1) + jnp.sum(tree_weights, axis=-1)
            weighted = jnp.einsum("ngt,td->ngd", cache_weights, cache_h[:, 1].astype(jnp.float32), precision=highest)
            weighted = weighted + jnp.einsum("ngj,jd->ngd", tree_weights, nodes_h[:, 1].astype(jnp.float32), precision=highest)
            return weighted / row_sum[..., None]

        heads_out = lax.map(per_head, (
            query_per_request.reshape(TREE_NODES, KEY_VALUE_HEADS, query_group_width, HEAD_WIDTH).transpose(1, 0, 2, 3),
            cache_per_request.transpose(1, 0, 2, 3),
            nodes_per_request.reshape(TREE_NODES, KEY_VALUE_HEADS, 2, HEAD_WIDTH).transpose(1, 0, 2, 3)))
        return heads_out.transpose(1, 0, 2, 3).reshape(TREE_NODES, QUERY_HEADS * HEAD_WIDTH)

    attention = lax.map(per_request, (queries, node_kv, global_table, tree_mask, lengths)).astype(jnp.bfloat16)
    projected = jnp.dot(attention.reshape(REQUEST_COUNT * TREE_NODES, QUERY_HEADS * HEAD_WIDTH), out_weight, preferred_element_type=jnp.float32).reshape(REQUEST_COUNT, TREE_NODES, D)

    ref_count = jnp.zeros((POOL_SLOTS,), jnp.int32).at[global_table.reshape(-1)].add(1)
    tail_page = (lengths // PAGE_ROWS).astype(jnp.int32)
    tail_owner = (tail_page // PPD).astype(jnp.int32)
    tail_slot = jnp.take_along_axis(global_table, tail_page[:, None], axis=1)[:, 0]
    shared = ref_count[tail_slot] > 1
    spare_local = jnp.take_along_axis(free_slot, tail_owner[:, None], axis=1)[:, 0]
    spare_global = (tail_owner * POOL_DEV + spare_local).astype(jnp.int32)
    copy_target = jnp.where(shared, spare_global, POOL_SLOTS).astype(jnp.int32)
    updated_pool = key_value_pool.at[copy_target].set(key_value_pool[tail_slot], mode="drop")
    page_hot = jnp.arange(PAGES, dtype=jnp.int32)[None, :] == tail_page[:, None]
    new_table = jnp.where(shared[:, None] & page_hot, spare_local[:, None], page_table).astype(jnp.int32)
    new_global = (owner_ids[None, :] * POOL_DEV + new_table).astype(jnp.int32)
    written_pool = jnp.take_along_axis(node_kv, accepted_path[:, :, None], axis=1)
    offsets = jnp.arange(PATH_ROWS, dtype=jnp.int32)
    row_pos = (lengths[:, None] + offsets[None, :]).astype(jnp.int32)
    row_live = offsets[None, :] < accept_count[:, None]
    row_page = (row_pos // PAGE_ROWS).astype(jnp.int32)
    row_pool_slot = jnp.where(row_live, jnp.take_along_axis(new_global, row_page, axis=1), POOL_SLOTS).astype(jnp.int32)
    row_within_page = (row_pos % PAGE_ROWS).astype(jnp.int32)
    updated_pool = updated_pool.at[row_pool_slot.reshape(-1), row_within_page.reshape(-1)].set(written_pool.reshape(REQUEST_COUNT * PATH_ROWS, 2 * KEY_VALUE_HEADS * HEAD_WIDTH), mode="drop")
    return (projected, updated_pool, new_table)
```

```python
import jax
import jax.numpy as jnp
from jax import lax
from jax.experimental import pallas as pl
from jax.experimental.pallas import tpu as pltpu
from jax.sharding import Mesh, PartitionSpec as P

F32 = jnp.float32
BF16 = jnp.bfloat16

HEAD = 128
PATH_ROWS = 8
PAGE = 64
REQUESTS = 8
HALF = 4
NODES = 64
PAGES_LOCAL = 8
SPAN = PAGE * PAGES_LOCAL
LANES = 8 * NODES
CHIPS = 32
TAIL = 8
BLOCK = 64 + TAIL
DEAD = -1e30
FLOOR = -1e28
LOG2E = 1.4426950408889634
SCALE2 = HEAD ** (-0.5) * LOG2E

W_ROWS = 512
PAGE_ROWS0 = W_ROWS
NODE_ROWS0 = W_ROWS + HALF * SPAN
SEND_ROWS = NODE_ROWS0 + 16

VMEM = pltpu.VMEM
SMEM = pltpu.SMEM
LIMIT = 40 * 1024 * 1024


def iota(shape, dim):
    return lax.broadcasted_iota(jnp.int32, shape, dim)


def dot(a, b, ca=1, cb=0):
    return lax.dot_general(a, b, (((ca,), (cb,)), ((), ())), preferred_element_type=F32)


def ctx_index():
    return (lax.axis_index("x") * 8 + lax.axis_index("y")) * 2 + lax.axis_index("core")


def pack_kernel(where, table, pool, weight, node, parents, send, mask, node_pad, sems):
    core = where[0]
    ctx = where[1]
    other = HALF * (1 - core)
    copies = []
    for r in range(HALF):
        for p in range(PAGES_LOCAL):
            n = r * PAGES_LOCAL + p
            copies.append(
                pltpu.make_async_copy(
                    pool.at[table[other + r, p]],
                    send.at[pl.ds(PAGE_ROWS0 + n * PAGE, PAGE), :],
                    sems.at[n],
                )
            )
    for half in range(2):
        copies.append(
            pltpu.make_async_copy(
                weight.at[pl.ds(half * W_ROWS, W_ROWS), :],
                send.at[pl.ds(0, W_ROWS), pl.ds(half * HEAD, HEAD)],
                sems.at[32 + half],
            )
        )
    for c in copies:
        c.start()
    rows = node[...].astype(F32)
    node_pad[...] = jnp.concatenate([rows, jnp.zeros_like(rows)], axis=0).astype(BF16)
    last = pltpu.make_async_copy(node_pad, send.at[pl.ds(NODE_ROWS0, 16), :], sems.at[34])
    last.start()
    up = iota((NODES, NODES), 0)
    down = iota((NODES, NODES), 1)
    twice = (iota((NODES, 2 * NODES), 0) == iota((NODES, 2 * NODES), 1) % NODES).astype(F32).astype(BF16)
    pick_row = iota((16, NODES), 0)
    pick_node = iota((16, NODES), 1)
    for r in range(HALF):
        mine = HALF * core + r
        link = parents[pl.ds(mine, 1), :]
        reach = ((up == link) | (up == down)).astype(F32).astype(BF16)
        for _ in range(6):
            reach = jnp.minimum(dot(reach, reach), 1.0).astype(BF16)
        pick = ((pick_row == mine) & (pick_node == ctx)) | (
            (pick_row == REQUESTS + mine) & (pick_node == ctx + 1 - 2 * core)
        )
        seen = dot(pick.astype(F32).astype(BF16), reach).astype(BF16)
        mask[r] = dot(seen, twice)
    for c in copies:
        c.wait()
    last.wait()


def attend_kernel(where, table, lengths, pool, queries, peer, node, mask, out, own, sems):
    core = where[0]
    ctx = where[1]
    mine = HALF * core
    copies = []
    for r in range(HALF):
        for p in range(PAGES_LOCAL):
            n = r * PAGES_LOCAL + p
            copies.append(
                pltpu.make_async_copy(
                    pool.at[table[mine + r, p]],
                    own.at[pl.ds(n * PAGE, PAGE), :],
                    sems.at[n],
                )
            )
    for c in copies:
        c.start()
    lane = iota((LANES, LANES), 1)
    order = (iota((LANES, LANES), 0) == (lane % NODES) * 8 + lane // NODES).astype(F32).astype(BF16)
    peer_node = peer[pl.ds(NODE_ROWS0, 16), :].astype(F32)[:REQUESTS]
    own_node = node[...].astype(F32)
    nodes = jnp.concatenate([own_node, peer_node], axis=0).astype(BF16)
    ones = jnp.ones((16, SPAN), BF16)
    ones_tree = jnp.ones((16, 16), BF16)
    row = iota((SPAN, LANES), 0)
    tail_row = iota((TAIL, HEAD), 0)
    for c in copies:
        c.wait()
    for r in range(HALF):
        part = queries[:, pl.ds((r // 2) * 16, 16), :].astype(F32)[:, (r % 2) * 8 : (r % 2) * 8 + 8, :]
        part = part.reshape(LANES, HEAD).astype(BF16)
        query = dot(part, order, 0, 0).astype(BF16)
        length = lengths[mine + r]
        span_own = own[pl.ds(r * SPAN, SPAN), :]
        span_peer = peer[pl.ds(PAGE_ROWS0 + r * SPAN, SPAN), :]
        live_own = row < length - ctx * SPAN
        live_peer = row < length - (ctx + 1 - 2 * core) * SPAN
        seen = jnp.concatenate([mask[r]] * 4, axis=1)
        s_own = jnp.where(live_own, dot(span_own[:, :HEAD], query), DEAD)
        s_peer = jnp.where(live_peer, dot(span_peer[:, :HEAD], query), DEAD)
        s_tree = jnp.where(seen > 0.5, dot(nodes[:, :HEAD], query), DEAD)
        peak = jnp.maximum(
            jnp.maximum(jnp.max(s_own, axis=0, keepdims=True), jnp.max(s_peer, axis=0, keepdims=True)),
            jnp.max(s_tree, axis=0, keepdims=True),
        )
        peak = jnp.maximum(peak, FLOOR) * SCALE2
        total = None
        for s, v, one in (
            (s_own, span_own[:, HEAD:], ones),
            (s_peer, span_peer[:, HEAD:], ones),
            (s_tree, nodes[:, HEAD:], ones_tree),
        ):
            p = jnp.exp2(s * SCALE2 - peak).astype(BF16)
            lhs = jnp.concatenate([v.astype(F32).T.astype(BF16), one], axis=0)
            add = dot(lhs, p)
            total = add if total is None else total + add
        row_sum = total[HEAD : HEAD + 1]
        some = row_sum > 0.0
        mixed = total[:HEAD] * (1.0 / jnp.where(some, row_sum, 1.0))
        log_sum = jnp.where(some, peak + jnp.log2(jnp.where(some, row_sum, 1.0)), DEAD)
        first = log_sum.astype(BF16).astype(F32)
        rest = log_sum - first
        second = rest.astype(BF16).astype(F32)
        third = rest - second
        for pair in range(4):
            lanes = slice(pair * HEAD, (pair + 1) * HEAD)
            for half in range(2):
                e = r * 8 + pair * 2 + half
                q = e // 4
                terms = (
                    first[:, lanes],
                    second[:, lanes],
                    third[:, lanes],
                    own_node[q : q + 1, :HEAD],
                    own_node[q : q + 1, HEAD:],
                    peer_node[q : q + 1, :HEAD],
                    peer_node[q : q + 1, HEAD:],
                )
                tail = jnp.zeros((TAIL, HEAD), F32)
                for t, term in enumerate(terms):
                    tail = jnp.where(tail_row == t, term, tail)
                block = jnp.concatenate([mixed[half * 64 : half * 64 + 64, lanes], tail], axis=0)
                out[e] = block.astype(BF16)


def combine_kernel(where, path, got, out):
    core = where[0]
    chip = where[1] // 2
    logs = []
    for s in range(CHIPS):
        tail = got[s].astype(F32)[64:BLOCK]
        logs.append(tail[0:1] + tail[1:2] + tail[2:3])
    peak = logs[0]
    for s in range(1, CHIPS):
        peak = jnp.maximum(peak, logs[s])
    total = jnp.zeros((1, HEAD), F32)
    mixed = jnp.zeros((64, HEAD), F32)
    for s in range(CHIPS):
        share = jnp.exp2(logs[s] - peak)
        total = total + share
        mixed = mixed + share * got[s].astype(F32)[:64]
    mixed = mixed * (1.0 / total)
    tail_row = iota((TAIL, HEAD), 0)
    tail = jnp.zeros((TAIL, HEAD), F32)
    for j in range(2):
        node = path[chip // 4, 2 * (chip % 4) + j]
        held = got[node // 2].astype(F32)[64:BLOCK]
        is_own = node % 2 == core
        key = jnp.where(is_own, held[3:4], held[5:6])
        value = jnp.where(is_own, held[4:5], held[6:7])
        tail = jnp.where(tail_row == 2 * j, key, tail)
        tail = jnp.where(tail_row == 2 * j + 1, value, tail)
    block = jnp.concatenate([mixed, tail], axis=0).astype(BF16)
    for s in range(CHIPS):
        out[s] = block


def project_kernel(where, got, weight, peer, out):
    core = where[0]
    own_w = weight[...]
    peer_w = peer[...]
    sides = []
    for h in range(2):
        own_h = jnp.concatenate([own_w[(2 * p + h) * HEAD : (2 * p + h + 1) * HEAD] for p in range(4)], axis=0)
        peer_h = []
        for p in range(4):
            at = (2 * p + h) * HEAD
            cols = slice((at // W_ROWS) * HEAD, (at // W_ROWS) * HEAD + HEAD)
            peer_h.append(peer_w[at % W_ROWS : at % W_ROWS + HEAD, cols])
        sides.append(jnp.concatenate([own_h, jnp.concatenate(peer_h, axis=0)], axis=1))
    for r in range(HALF):
        a = got[pl.ds(r * 8, 8)][:, :64, :].reshape(W_ROWS, HEAD)
        even = dot(a, sides[0], 0, 0)
        odd = dot(a, sides[1], 0, 0)
        sums = even[:NODES] + odd[NODES:]
        for t in range(8):
            out[core * 8 + t, r] = sums[t * 8 : t * 8 + 8, :HEAD]
            out[(1 - core) * 8 + t, r] = sums[t * 8 : t * 8 + 8, HEAD:]


def write_kernel(where, table, lengths, counts, spare, table_v, got, pool_in, pool, new_table, pages, sems):
    ctx = where[1]
    for r in range(REQUESTS):
        for p in range(PAGES_LOCAL):
            new_table[r, p] = table[r, p]
    row = iota((PAGE, 2 * HEAD), 0)
    for r in range(REQUESTS):
        length = lengths[r]
        count = counts[r]
        tail_page = length // PAGE
        for step in range(2):
            page = tail_page + step
            local = page - ctx * PAGES_LOCAL
            first = length - page * PAGE
            here = (local >= 0) & (local < PAGES_LOCAL)
            if step == 1:
                here = here & (first + count > 0)

            @pl.when(here)
            def _():
                slot = table[r, local]
                target = slot
                if step == 0:
                    uses = jnp.sum((table_v[...] == slot).astype(jnp.int32))
                    target = jnp.where(uses > 1, spare[r, 0], slot)
                    new_table[r, local] = target
                fetch = pltpu.make_async_copy(pool_in.at[slot], pages.at[2 * r + step], sems.at[2 * r + step])
                fetch.start()
                fetch.wait()
                now = pages[2 * r + step].astype(F32)
                for j in range(PATH_ROWS):
                    held = got[r * 4 + j // 2].astype(F32)[64:BLOCK]
                    new = jnp.concatenate([held[2 * (j % 2) : 2 * (j % 2) + 1], held[2 * (j % 2) + 1 : 2 * (j % 2) + 2]], axis=1)
                    now = jnp.where((row == first + j) & (j < count), new, now)
                pages[2 * r + step] = now.astype(BF16)
                store = pltpu.make_async_copy(pages.at[2 * r + step], pool.at[target], sems.at[2 * r + step])
                store.start()
                store.wait()


def spec(space):
    return pl.BlockSpec(memory_space=space)


def on_device(queries, node_kv, pool, out_weight, parents, path, counts, lengths, table, free_slot):
    params = pltpu.CompilerParams(vmem_limit_bytes=LIMIT)
    any_ = spec(pl.ANY)
    core = lax.axis_index("core")
    where = jnp.stack([core, ctx_index()]).astype(jnp.int32)
    node = node_kv.reshape(REQUESTS, 2 * HEAD)

    send, mask = pl.pallas_call(
        pack_kernel,
        out_shape=(
            jax.ShapeDtypeStruct((SEND_ROWS, 2 * HEAD), BF16),
            jax.ShapeDtypeStruct((HALF, 16, 2 * NODES), F32),
        ),
        in_specs=[spec(SMEM), spec(SMEM), any_, any_, spec(VMEM), spec(VMEM)],
        out_specs=(any_, spec(VMEM)),
        scratch_shapes=[VMEM((16, 2 * HEAD), BF16), pltpu.SemaphoreType.DMA((35,))],
        compiler_params=params,
        name="pack",
    )(where, table, pool, out_weight, node, parents)
    peer = lax.ppermute(send, "core", [(0, 1), (1, 0)])

    by_core = queries.reshape(2, HALF * 8, HEAD)
    message = jnp.broadcast_to(by_core[None], (CHIPS, 2, HALF * 8, HEAD)).reshape(2 * CHIPS, HALF * 8, HEAD)
    every_query = lax.all_to_all(message, ("x", "y", "core"), 0, 0, tiled=True)

    partial = pl.pallas_call(
        attend_kernel,
        out_shape=jax.ShapeDtypeStruct((CHIPS, BLOCK, HEAD), BF16),
        in_specs=[spec(SMEM), spec(SMEM), spec(SMEM), any_, spec(VMEM), spec(VMEM), spec(VMEM), spec(VMEM)],
        out_specs=spec(VMEM),
        scratch_shapes=[VMEM((HALF * SPAN, 2 * HEAD), BF16), pltpu.SemaphoreType.DMA((32,))],
        compiler_params=params,
        name="attend",
    )(where, table, lengths, pool, every_query, peer, node, mask)

    parts = lax.all_to_all(partial, ("x", "y"), 0, 0, tiled=True)
    mixed = pl.pallas_call(
        combine_kernel,
        out_shape=jax.ShapeDtypeStruct((CHIPS, BLOCK, HEAD), BF16),
        in_specs=[spec(SMEM), spec(SMEM), spec(VMEM)],
        out_specs=spec(VMEM),
        compiler_params=params,
        name="combine",
    )(where, path, parts)
    attention = lax.all_to_all(mixed, ("x", "y"), 0, 0, tiled=True)

    sums = pl.pallas_call(
        project_kernel,
        grid=(1,),
        out_shape=jax.ShapeDtypeStruct((16, HALF, 8, HEAD), F32),
        in_specs=[
            spec(SMEM),
            pl.BlockSpec((CHIPS, BLOCK, HEAD), lambda i: (0, 0, 0)),
            pl.BlockSpec((8 * HEAD, HEAD), lambda i: (0, 0)),
            pl.BlockSpec((W_ROWS, 2 * HEAD), lambda i: (0, 0)),
        ],
        out_specs=pl.BlockSpec((16, HALF, 8, HEAD), lambda i: (0, 0, 0, 0)),
        compiler_params=params,
        name="project",
    )(where, attention, out_weight, peer)
    shares = lax.all_to_all(sums, ("core", "tp"), 0, 0, tiled=True)
    projected = jnp.sum(shares.reshape(2, 8, HALF, 8, HEAD), axis=1).reshape(REQUESTS, 8, HEAD)

    updated_pool, new_table = pl.pallas_call(
        write_kernel,
        out_shape=(
            jax.ShapeDtypeStruct(pool.shape, pool.dtype),
            jax.ShapeDtypeStruct(table.shape, table.dtype),
        ),
        in_specs=[spec(SMEM)] * 5 + [spec(VMEM), spec(VMEM), any_],
        out_specs=(any_, spec(SMEM)),
        input_output_aliases={7: 0},
        scratch_shapes=[VMEM((2 * REQUESTS, PAGE, 2 * HEAD), BF16), pltpu.SemaphoreType.DMA((2 * REQUESTS,))],
        compiler_params=params,
        name="write",
    )(where, table, lengths, counts, free_slot, table, attention, pool)
    return projected, updated_pool, new_table


def solution(mesh):
    fine = Mesh(mesh.devices.reshape(4, 8, 2, 8), ("x", "y", "core", "tp"))
    ctx = ("x", "y", "core")
    placed = (
        P(None, ctx, "tp"),
        P(None, ctx, "tp"),
        P(ctx, None, "tp"),
        P("tp", ctx),
        P(),
        P(),
        P(),
        P(),
        P(None, ctx),
        P(None, ctx),
    )
    return jax.shard_map(
        on_device,
        mesh=fine,
        in_specs=placed,
        out_specs=(P(None, "tp", ctx), P(ctx, None, "tp"), P(None, ctx)),
        check_vma=False,
    )
```

```python
import jax
import jax.numpy as jnp
from jax import lax
from jax.experimental import pallas as pl
from jax.experimental.pallas import tpu as pltpu
from jax.sharding import Mesh, PartitionSpec as P

F32 = jnp.float32
BF16 = jnp.bfloat16

HEAD = 128
PATH_ROWS = 8
PAGE = 64
REQUESTS = 8
HALF = 4
NODES = 64
PAGES_LOCAL = 8
SPAN = PAGE * PAGES_LOCAL
LANES = 8 * NODES
CHIPS = 32
TAIL = 8
BLOCK = 64 + TAIL
GATHERED = 64 + 2 * PATH_ROWS
NEIGHBOURS = 8
DEAD = -1e30
FLOOR = -1e28
LOG2E = 1.4426950408889634
SCALE2 = HEAD ** (-0.5) * LOG2E

NODE_ROWS0 = HALF * SPAN
SEND_ROWS = NODE_ROWS0 + 16

VMEM = pltpu.VMEM
SMEM = pltpu.SMEM
HBM = pltpu.HBM
LIMIT = 40 * 1024 * 1024


def iota(shape, dim):
    return lax.broadcasted_iota(jnp.int32, shape, dim)


def dot(a, b, ca=1, cb=0):
    return lax.dot_general(a, b, (((ca,), (cb,)), ((), ())), preferred_element_type=F32)


def ctx_index():
    return (lax.axis_index("x") * 8 + lax.axis_index("y")) * 2 + lax.axis_index("core")


def pack_kernel(where, table, pool, node, send, node_pad, sems):
    other = HALF * (1 - where[0])
    copies = []
    for r in range(HALF):
        for p in range(PAGES_LOCAL):
            n = r * PAGES_LOCAL + p
            copies.append(
                pltpu.make_async_copy(
                    pool.at[table[other + r, p]], send.at[pl.ds(n * PAGE, PAGE), :], sems.at[n]
                )
            )
    for c in copies:
        c.start()
    rows = node[...].astype(F32)
    node_pad[...] = jnp.concatenate([rows, jnp.zeros_like(rows)], axis=0).astype(BF16)
    last = pltpu.make_async_copy(node_pad, send.at[pl.ds(NODE_ROWS0, 16), :], sems.at[32])
    last.start()
    for c in copies:
        c.wait()
    last.wait()


def prepare_kernel(where, table, pool, parents, own, pool_copy, mask, sems):
    core = where[0]
    ctx = where[1]
    copies = []
    for r in range(HALF):
        for p in range(PAGES_LOCAL):
            n = r * PAGES_LOCAL + p
            copies.append(
                pltpu.make_async_copy(
                    pool.at[table[HALF * core + r, p]], own.at[pl.ds(n * PAGE, PAGE), :], sems.at[n]
                )
            )
    copies.append(pltpu.make_async_copy(pool, pool_copy, sems.at[32]))
    for c in copies:
        c.start()
    up = iota((NODES, NODES), 0)
    down = iota((NODES, NODES), 1)
    twice = (iota((NODES, 2 * NODES), 0) == iota((NODES, 2 * NODES), 1) % NODES).astype(F32).astype(BF16)
    pick_row = iota((16, NODES), 0)
    pick_node = iota((16, NODES), 1)
    reach = []
    for r in range(HALF):
        link = parents[pl.ds(HALF * core + r, 1), :]
        reach.append(((up == link) | (up == down)).astype(F32).astype(BF16))
    for _ in range(6):
        reach = [jnp.minimum(dot(m, m), 1.0).astype(BF16) for m in reach]
    for r in range(HALF):
        mine = HALF * core + r
        pick = ((pick_row == mine) & (pick_node == ctx)) | (
            (pick_row == REQUESTS + mine) & (pick_node == ctx + 1 - 2 * core)
        )
        seen = dot(pick.astype(F32).astype(BF16), reach[r]).astype(BF16)
        mask[r] = dot(seen, twice)
    for c in copies:
        c.wait()


def attend_kernel(where, lengths, queries, own, peer, node, mask, out):
    core = where[0]
    ctx = where[1]
    lane = iota((LANES, LANES), 1)
    order = (iota((LANES, LANES), 0) == (lane % NODES) * 8 + lane // NODES).astype(F32).astype(BF16)
    peer_node = peer[pl.ds(NODE_ROWS0, 16), :].astype(F32)[:REQUESTS]
    own_node = node[...].astype(F32)
    nodes = jnp.concatenate([own_node, peer_node], axis=0).astype(BF16)
    ones = jnp.ones((16, SPAN), BF16)
    ones_tree = jnp.ones((16, 16), BF16)
    row = iota((SPAN, LANES), 0)
    tail_row = iota((TAIL, HEAD), 0)
    for r in range(HALF):
        part = queries[:, pl.ds((r // 2) * 16, 16), :].astype(F32)[:, (r % 2) * 8 : (r % 2) * 8 + 8, :]
        part = part.reshape(LANES, HEAD).astype(BF16)
        query = dot(part, order, 0, 0).astype(BF16)
        length = lengths[HALF * core + r]
        span_own = own[pl.ds(r * SPAN, SPAN), :]
        span_peer = peer[pl.ds(r * SPAN, SPAN), :]
        live_own = row < length - ctx * SPAN
        live_peer = row < length - (ctx + 1 - 2 * core) * SPAN
        seen = jnp.concatenate([mask[r]] * 4, axis=1)
        s_own = jnp.where(live_own, dot(span_own[:, :HEAD], query), DEAD)
        s_peer = jnp.where(live_peer, dot(span_peer[:, :HEAD], query), DEAD)
        s_tree = jnp.where(seen > 0.5, dot(nodes[:, :HEAD], query), DEAD)
        peak = jnp.maximum(
            jnp.maximum(jnp.max(s_own, axis=0, keepdims=True), jnp.max(s_peer, axis=0, keepdims=True)),
            jnp.max(s_tree, axis=0, keepdims=True),
        )
        peak = jnp.maximum(peak, FLOOR) * SCALE2
        total = None
        for s, v, one in (
            (s_own, span_own[:, HEAD:], ones),
            (s_peer, span_peer[:, HEAD:], ones),
            (s_tree, nodes[:, HEAD:], ones_tree),
        ):
            p = jnp.exp2(s * SCALE2 - peak)
            lhs = jnp.concatenate([v.astype(F32).T.astype(BF16), one], axis=0)
            high = p.astype(BF16)
            low = (p - high.astype(F32)).astype(BF16)
            add = dot(lhs, high) + dot(lhs, low)
            total = add if total is None else total + add
        row_sum = total[HEAD : HEAD + 1]
        some = row_sum > 0.0
        mixed = total[:HEAD] * (1.0 / jnp.where(some, row_sum, 1.0))
        log_sum = jnp.where(some, peak + jnp.log2(jnp.where(some, row_sum, 1.0)), DEAD)
        first = log_sum.astype(BF16).astype(F32)
        rest = log_sum - first
        second = rest.astype(BF16).astype(F32)
        third = rest - second
        for y in range(8):
            lanes = slice((y // 2) * HEAD, (y // 2 + 1) * HEAD)
            half = y % 2
            terms = (
                first[:, lanes],
                second[:, lanes],
                third[:, lanes],
                own_node[y : y + 1, :HEAD],
                own_node[y : y + 1, HEAD:],
                peer_node[y : y + 1, :HEAD],
                peer_node[y : y + 1, HEAD:],
            )
            tail = jnp.zeros((TAIL, HEAD), F32)
            for t, term in enumerate(terms):
                tail = jnp.where(tail_row == t, term, tail)
            block = jnp.concatenate([mixed[half * 64 : half * 64 + 64, lanes], tail], axis=0)
            out[r * 8 + y] = block.astype(BF16)


def combine_kernel(where, path, got, out):
    core = where[0]
    y = (where[1] // 2) % 8
    logs = []
    for s in range(CHIPS):
        tail = got[s].astype(F32)[64:BLOCK]
        logs.append(tail[0:1] + tail[1:2] + tail[2:3])
    peak = logs[0]
    for s in range(1, CHIPS):
        peak = jnp.maximum(peak, logs[s])
    total = jnp.zeros((1, HEAD), F32)
    mixed = jnp.zeros((64, HEAD), F32)
    for s in range(CHIPS):
        share = jnp.exp2(logs[s] - peak)
        total = total + share
        mixed = mixed + share * got[s].astype(F32)[:64]
    mixed = mixed * (1.0 / total)
    tail_row = iota((2 * PATH_ROWS, HEAD), 0)
    tail = jnp.zeros((2 * PATH_ROWS, HEAD), F32)
    for j in range(PATH_ROWS):
        node = path[y, j]
        held = got[node // 2].astype(F32)[64:BLOCK]
        is_own = node % 2 == core
        key = jnp.where(is_own, held[3:4], held[5:6])
        value = jnp.where(is_own, held[4:5], held[6:7])
        tail = jnp.where(tail_row == 2 * j, key, tail)
        tail = jnp.where(tail_row == 2 * j + 1, value, tail)
    block = jnp.concatenate([mixed, tail], axis=0).astype(BF16)
    for s in range(8):
        out[s] = block


def project_kernel(got, weights, out):
    a = got[...][:, :64, :].reshape(LANES, HEAD)
    for pair in range(NEIGHBOURS // 2):
        sums = None
        for h in range(2):
            cols = []
            for n in (2 * pair, 2 * pair + 1):
                rows = [weights[n, (2 * p + h) * HEAD : (2 * p + h + 1) * HEAD, :] for p in range(4)]
                cols.append(jnp.concatenate(rows, axis=0))
            part = dot(a, jnp.concatenate(cols, axis=1), 0, 0)[h * NODES : (h + 1) * NODES]
            sums = part if sums is None else sums + part
        for t in range(8):
            rows = sums[t * 8 : t * 8 + 8]
            out[2 * pair * 8 + t] = rows[:, :HEAD]
            out[(2 * pair + 1) * 8 + t] = rows[:, HEAD:]


def write_kernel(where, table, lengths, counts, spare, table_v, got, pool_in, pool, new_table, pages, sems):
    ctx = where[1]
    for r in range(REQUESTS):
        for p in range(PAGES_LOCAL):
            new_table[r, p] = table[r, p]
    row = iota((PAGE, 2 * HEAD), 0)
    for r in range(REQUESTS):
        length = lengths[r]
        count = counts[r]
        tail_page = length // PAGE
        for step in range(2):
            page = tail_page + step
            local = page - ctx * PAGES_LOCAL
            first = length - page * PAGE
            here = (local >= 0) & (local < PAGES_LOCAL)
            if step == 1:
                here = here & (first + count > 0)

            @pl.when(here)
            def _():
                slot = table[r, local]
                target = slot
                if step == 0:
                    uses = jnp.sum((table_v[...] == slot).astype(jnp.int32))
                    target = jnp.where(uses > 1, spare[r, 0], slot)
                    new_table[r, local] = target
                fetch = pltpu.make_async_copy(pool_in.at[slot], pages.at[2 * r + step], sems.at[2 * r + step])
                fetch.start()
                fetch.wait()
                now = pages[2 * r + step].astype(F32)
                held = got[r].astype(F32)[64:GATHERED]
                for j in range(PATH_ROWS):
                    new = jnp.concatenate([held[2 * j : 2 * j + 1], held[2 * j + 1 : 2 * j + 2]], axis=1)
                    now = jnp.where((row == first + j) & (j < count), new, now)
                pages[2 * r + step] = now.astype(BF16)
                store = pltpu.make_async_copy(pages.at[2 * r + step], pool.at[target], sems.at[2 * r + step])
                store.start()
                store.wait()


def spec(space):
    return pl.BlockSpec(memory_space=space)


def on_device(queries, node_kv, pool, out_weight, parents, path, counts, lengths, table, free_slot):
    params = pltpu.CompilerParams(vmem_limit_bytes=LIMIT)
    shape = jax.ShapeDtypeStruct
    where = jnp.stack([lax.axis_index("core"), ctx_index()]).astype(jnp.int32)
    node = node_kv.reshape(REQUESTS, 2 * HEAD)
    weights = lax.all_gather(out_weight, ("x", "core"), axis=0)

    send = pl.pallas_call(
        pack_kernel,
        out_shape=shape((SEND_ROWS, 2 * HEAD), BF16),
        in_specs=[spec(SMEM), spec(SMEM), spec(HBM), spec(VMEM)],
        out_specs=spec(pl.ANY),
        scratch_shapes=[VMEM((16, 2 * HEAD), BF16), pltpu.SemaphoreType.DMA((33,))],
        compiler_params=params,
        name="pack",
    )(where, table, pool, node)
    peer = lax.ppermute(send, "core", [(0, 1), (1, 0)])

    by_core = queries.reshape(2, HALF * 8, HEAD)
    message = jnp.broadcast_to(by_core[None], (CHIPS, 2, HALF * 8, HEAD)).reshape(2 * CHIPS, HALF * 8, HEAD)
    every_query = lax.all_to_all(message, ("x", "y", "core"), 0, 0, tiled=True)

    own, pool_copy, mask = pl.pallas_call(
        prepare_kernel,
        out_shape=(
            shape((HALF * SPAN, 2 * HEAD), BF16),
            shape(pool.shape, pool.dtype),
            shape((HALF, 16, 2 * NODES), F32),
        ),
        in_specs=[spec(SMEM), spec(SMEM), spec(HBM), spec(VMEM)],
        out_specs=(spec(VMEM), spec(HBM), spec(VMEM)),
        scratch_shapes=[pltpu.SemaphoreType.DMA((33,))],
        compiler_params=params,
        cost_estimate=pl.CostEstimate(flops=50_000_000, bytes_accessed=7_000_000, transcendentals=0),
        name="prepare",
    )(where, table, pool, parents)

    partial = pl.pallas_call(
        attend_kernel,
        out_shape=shape((CHIPS, BLOCK, HEAD), BF16),
        in_specs=[spec(SMEM), spec(SMEM)] + [spec(VMEM)] * 5,
        out_specs=spec(VMEM),
        compiler_params=params,
        name="attend",
    )(where, lengths, every_query, own, peer, node, mask)

    parts = lax.all_to_all(partial, ("x", "y"), 0, 0, tiled=True)
    mixed = pl.pallas_call(
        combine_kernel,
        out_shape=shape((8, GATHERED, HEAD), BF16),
        in_specs=[spec(SMEM), spec(SMEM), spec(VMEM)],
        out_specs=spec(VMEM),
        compiler_params=params,
        name="combine",
    )(where, path, parts)
    attention = lax.all_to_all(mixed, "y", 0, 0, tiled=True)

    sums = pl.pallas_call(
        project_kernel,
        out_shape=shape((64, 8, HEAD), F32),
        in_specs=[spec(VMEM), spec(VMEM)],
        out_specs=spec(VMEM),
        compiler_params=params,
        name="project",
    )(attention, weights)
    shares = lax.all_to_all(sums, ("x", "core", "tp"), 0, 0, tiled=True)
    summed = jnp.sum(shares.reshape(4, 2, 8, 8, HEAD), axis=2)
    projected = jnp.swapaxes(summed, 0, 1).reshape(REQUESTS, 8, HEAD)

    updated_pool, new_table = pl.pallas_call(
        write_kernel,
        out_shape=(shape(pool.shape, pool.dtype), shape(table.shape, table.dtype)),
        in_specs=[spec(SMEM)] * 5 + [spec(VMEM), spec(VMEM), spec(HBM)],
        out_specs=(spec(HBM), spec(SMEM)),
        input_output_aliases={7: 0},
        scratch_shapes=[VMEM((2 * REQUESTS, PAGE, 2 * HEAD), BF16), pltpu.SemaphoreType.DMA((2 * REQUESTS,))],
        compiler_params=params,
        name="write",
    )(where, table, lengths, counts, free_slot, table, attention, pool_copy)
    return projected, updated_pool, new_table


def solution(mesh):
    fine = Mesh(mesh.devices.reshape(4, 8, 2, 8), ("x", "y", "core", "tp"))
    ctx = ("x", "y", "core")
    placed = (
        P(None, ctx, "tp"),
        P(None, ctx, "tp"),
        P(ctx, None, "tp"),
        P("tp", ctx),
        P(),
        P(),
        P(),
        P(),
        P(None, ctx),
        P(None, ctx),
    )
    return jax.shard_map(
        on_device,
        mesh=fine,
        in_specs=placed,
        out_specs=(P(None, "tp", ctx), P(ctx, None, "tp"), P(None, ctx)),
        check_vma=False,
    )
```

```python
import jax
import jax.numpy as jnp
from jax import lax
from jax.experimental import pallas as pl
from jax.experimental.pallas import tpu as pltpu
from jax.sharding import Mesh, PartitionSpec as P

F32 = jnp.float32
BF16 = jnp.bfloat16

HEAD = 128
PATH_ROWS = 8
PAGE = 64
REQUESTS = 8
HALF = 4
NODES = 64
PAGES_LOCAL = 8
SPAN = PAGE * PAGES_LOCAL
LANES = 8 * NODES
CHIPS = 32
TAIL = 8
BLOCK = 64 + TAIL
NEIGHBOURS = 4
DEAD = -1e30
FLOOR = -1e28
LOG2E = 1.4426950408889634
SCALE2 = HEAD ** (-0.5) * LOG2E

NODE_ROWS0 = HALF * SPAN
SEND_ROWS = NODE_ROWS0 + 16

VMEM = pltpu.VMEM
SMEM = pltpu.SMEM
HBM = pltpu.HBM
LIMIT = 40 * 1024 * 1024


def iota(shape, dim):
    return lax.broadcasted_iota(jnp.int32, shape, dim)


def dot(a, b, ca=1, cb=0):
    return lax.dot_general(a, b, (((ca,), (cb,)), ((), ())), preferred_element_type=F32)


def ctx_index():
    return (lax.axis_index("x") * 8 + lax.axis_index("y")) * 2 + lax.axis_index("core")


def pack_kernel(where, table, pool, node, query, send, message, node_pad, sems):
    other = HALF * (1 - where[0])
    copies = []
    for r in range(HALF):
        for p in range(PAGES_LOCAL):
            n = r * PAGES_LOCAL + p
            copies.append(
                pltpu.make_async_copy(
                    pool.at[table[other + r, p]], send.at[pl.ds(n * PAGE, PAGE), :], sems.at[n]
                )
            )
    for c in copies:
        c.start()
    rows = node[...].astype(F32)
    node_pad[...] = jnp.concatenate([rows, jnp.zeros_like(rows)], axis=0).astype(BF16)
    last = pltpu.make_async_copy(node_pad, send.at[pl.ds(NODE_ROWS0, 16), :], sems.at[32])
    last.start()
    for half in range(2):
        rows = query[half]
        for chip in range(CHIPS):
            message[2 * chip + half] = rows
    for c in copies:
        c.wait()
    last.wait()


def prepare_kernel(where, table, pool, parents, own, pool_copy, mask, sems):
    core = where[0]
    ctx = where[1]
    copies = []
    for r in range(HALF):
        for p in range(PAGES_LOCAL):
            n = r * PAGES_LOCAL + p
            copies.append(
                pltpu.make_async_copy(
                    pool.at[table[HALF * core + r, p]], own.at[pl.ds(n * PAGE, PAGE), :], sems.at[n]
                )
            )
    copies.append(pltpu.make_async_copy(pool, pool_copy, sems.at[32]))
    for c in copies:
        c.start()
    up = iota((NODES, NODES), 0)
    down = iota((NODES, NODES), 1)
    twice = (iota((NODES, 2 * NODES), 0) == iota((NODES, 2 * NODES), 1) % NODES).astype(F32).astype(BF16)
    pick_row = iota((16, NODES), 0)
    pick_node = iota((16, NODES), 1)
    reach = []
    for r in range(HALF):
        link = parents[pl.ds(HALF * core + r, 1), :]
        reach.append(((up == link) | (up == down)).astype(F32).astype(BF16))
    for _ in range(6):
        reach = [jnp.minimum(dot(m, m), 1.0).astype(BF16) for m in reach]
    for r in range(HALF):
        mine = HALF * core + r
        pick = ((pick_row == mine) & (pick_node == ctx)) | (
            (pick_row == REQUESTS + mine) & (pick_node == ctx + 1 - 2 * core)
        )
        seen = dot(pick.astype(F32).astype(BF16), reach[r]).astype(BF16)
        mask[r] = dot(seen, twice)
    for c in copies:
        c.wait()


def attend_kernel(where, lengths, queries, own, peer, node, mask, out):
    core = where[0]
    ctx = where[1]
    lane = iota((LANES, LANES), 1)
    order = (iota((LANES, LANES), 0) == (lane % NODES) * 8 + lane // NODES).astype(F32).astype(BF16)
    peer_node = peer[pl.ds(NODE_ROWS0, 16), :].astype(F32)[:REQUESTS]
    own_node = node[...].astype(F32)
    nodes = jnp.concatenate([own_node, peer_node], axis=0).astype(BF16)
    ones = jnp.ones((16, SPAN), BF16)
    ones_tree = jnp.ones((16, 16), BF16)
    row = iota((SPAN, LANES), 0)
    tail_row = iota((TAIL, HEAD), 0)
    for r in range(HALF):
        part = queries[:, pl.ds((r // 2) * 16, 16), :].astype(F32)[:, (r % 2) * 8 : (r % 2) * 8 + 8, :]
        part = part.reshape(LANES, HEAD).astype(BF16)
        query = dot(part, order, 0, 0).astype(BF16)
        length = lengths[HALF * core + r]
        span_own = own[pl.ds(r * SPAN, SPAN), :]
        span_peer = peer[pl.ds(r * SPAN, SPAN), :]
        live_own = row < length - ctx * SPAN
        live_peer = row < length - (ctx + 1 - 2 * core) * SPAN
        seen = jnp.concatenate([mask[r]] * 4, axis=1)
        s_own = jnp.where(live_own, dot(span_own[:, :HEAD], query), DEAD)
        s_peer = jnp.where(live_peer, dot(span_peer[:, :HEAD], query), DEAD)
        s_tree = jnp.where(seen > 0.5, dot(nodes[:, :HEAD], query), DEAD)
        peak = jnp.maximum(
            jnp.maximum(jnp.max(s_own, axis=0, keepdims=True), jnp.max(s_peer, axis=0, keepdims=True)),
            jnp.max(s_tree, axis=0, keepdims=True),
        )
        peak = jnp.maximum(peak, FLOOR) * SCALE2
        total = None
        for s, v, one in (
            (s_own, span_own[:, HEAD:], ones),
            (s_peer, span_peer[:, HEAD:], ones),
            (s_tree, nodes[:, HEAD:], ones_tree),
        ):
            p = jnp.exp2(s * SCALE2 - peak)
            lhs = jnp.concatenate([v.astype(F32).T.astype(BF16), one], axis=0)
            high = p.astype(BF16)
            low = (p - high.astype(F32)).astype(BF16)
            add = dot(lhs, high) + dot(lhs, low)
            total = add if total is None else total + add
        row_sum = total[HEAD : HEAD + 1]
        some = row_sum > 0.0
        mixed = total[:HEAD] * (1.0 / jnp.where(some, row_sum, 1.0))
        log_sum = jnp.where(some, peak + jnp.log2(jnp.where(some, row_sum, 1.0)), DEAD)
        first = log_sum.astype(BF16).astype(F32)
        rest = log_sum - first
        second = rest.astype(BF16).astype(F32)
        third = rest - second
        for y in range(8):
            lanes = slice((y // 2) * HEAD, (y // 2 + 1) * HEAD)
            half = y % 2
            terms = (
                first[:, lanes],
                second[:, lanes],
                third[:, lanes],
                own_node[y : y + 1, :HEAD],
                own_node[y : y + 1, HEAD:],
                peer_node[y : y + 1, :HEAD],
                peer_node[y : y + 1, HEAD:],
            )
            tail = jnp.zeros((TAIL, HEAD), F32)
            for t, term in enumerate(terms):
                tail = jnp.where(tail_row == t, term, tail)
            block = jnp.concatenate([mixed[half * 64 : half * 64 + 64, lanes], tail], axis=0)
            out[r * 8 + y] = block.astype(BF16)


def combine_kernel(where, path, got, out):
    core = where[0]
    y = (where[1] // 2) % 8
    logs = []
    for s in range(CHIPS):
        tail = got[s].astype(F32)[64:BLOCK]
        logs.append(tail[0:1] + tail[1:2] + tail[2:3])
    peak = logs[0]
    for s in range(1, CHIPS):
        peak = jnp.maximum(peak, logs[s])
    total = jnp.zeros((1, HEAD), F32)
    mixed = jnp.zeros((64, HEAD), F32)
    for s in range(CHIPS):
        share = jnp.exp2(logs[s] - peak)
        total = total + share
        mixed = mixed + share * got[s].astype(F32)[:64]
    mixed = mixed * (1.0 / total)
    tail_row = iota((TAIL, HEAD), 0)
    tail = jnp.zeros((TAIL, HEAD), F32)
    for j in range(HALF):
        node = path[y, HALF * core + j]
        held = got[node // 2].astype(F32)[64:BLOCK]
        is_own = node % 2 == core
        key = jnp.where(is_own, held[3:4], held[5:6])
        value = jnp.where(is_own, held[4:5], held[6:7])
        tail = jnp.where(tail_row == 2 * j, key, tail)
        tail = jnp.where(tail_row == 2 * j + 1, value, tail)
    block = jnp.concatenate([mixed, tail], axis=0).astype(BF16)
    for s in range(16):
        out[s] = block


def project_kernel(where, got, w0, w1, w2, w3, out):
    x = where[1] // 16
    held = got[...].reshape(8, 2, BLOCK, HEAD)
    weights = (w0, w1, w2, w3)
    for pair in range(NEIGHBOURS // 2):
        wide = []
        for h in range(2):
            cols = []
            for n in (2 * pair, 2 * pair + 1):
                rows = [weights[n][(2 * p + h) * HEAD : (2 * p + h + 1) * HEAD, :] for p in range(4)]
                cols.append(jnp.concatenate(rows, axis=0))
            wide.append(jnp.concatenate(cols, axis=1))
        for k in range(2):
            a = held[:, k, :64, :].reshape(LANES, HEAD)
            sums = dot(a, wide[0], 0, 0)[:NODES] + dot(a, wide[1], 0, 0)[NODES:]
            for n in range(2):
                to = lax.rem(x + 2 * pair + n, NEIGHBOURS)
                for t in range(8):
                    out[to * 8 + t, k] = sums[t * 8 : t * 8 + 8, n * HEAD : (n + 1) * HEAD]


def sum_kernel(got, out):
    for x in range(NEIGHBOURS):
        total = got[x * 8]
        for t in range(1, 8):
            total = total + got[x * 8 + t]
        out[x] = total[0]
        out[HALF + x] = total[1]


def write_kernel(where, table, lengths, counts, spare, table_v, got, pool_in, pool, new_table, pages, sems):
    ctx = where[1]
    for r in range(REQUESTS):
        for p in range(PAGES_LOCAL):
            new_table[r, p] = table[r, p]
    row = iota((PAGE, 2 * HEAD), 0)
    for r in range(REQUESTS):
        length = lengths[r]
        count = counts[r]
        tail_page = length // PAGE
        for step in range(2):
            page = tail_page + step
            local = page - ctx * PAGES_LOCAL
            first = length - page * PAGE
            here = (local >= 0) & (local < PAGES_LOCAL)
            if step == 1:
                here = here & (first + count > 0)

            @pl.when(here)
            def _():
                slot = table[r, local]
                target = slot
                if step == 0:
                    uses = jnp.sum((table_v[...] == slot).astype(jnp.int32))
                    target = jnp.where(uses > 1, spare[r, 0], slot)
                    new_table[r, local] = target
                fetch = pltpu.make_async_copy(pool_in.at[slot], pages.at[2 * r + step], sems.at[2 * r + step])
                fetch.start()
                fetch.wait()
                now = pages[2 * r + step].astype(F32)
                for j in range(PATH_ROWS):
                    held = got[2 * r + j // HALF].astype(F32)[64:BLOCK]
                    at = 2 * (j % HALF)
                    new = jnp.concatenate([held[at : at + 1], held[at + 1 : at + 2]], axis=1)
                    now = jnp.where((row == first + j) & (j < count), new, now)
                pages[2 * r + step] = now.astype(BF16)
                store = pltpu.make_async_copy(pages.at[2 * r + step], pool.at[target], sems.at[2 * r + step])
                store.start()
                store.wait()


def spec(space):
    return pl.BlockSpec(memory_space=space)


def on_device(queries, node_kv, pool, out_weight, parents, path, counts, lengths, table, free_slot):
    params = pltpu.CompilerParams(vmem_limit_bytes=LIMIT)
    shape = jax.ShapeDtypeStruct
    where = jnp.stack([lax.axis_index("core"), ctx_index()]).astype(jnp.int32)
    node = node_kv.reshape(REQUESTS, 2 * HEAD)
    held_pool = pltpu.with_memory_space_constraint(pool, HBM)

    send, message = pl.pallas_call(
        pack_kernel,
        out_shape=(shape((SEND_ROWS, 2 * HEAD), BF16), shape((2 * CHIPS, HALF * 8, HEAD), BF16)),
        in_specs=[spec(SMEM), spec(SMEM), spec(HBM), spec(VMEM), spec(VMEM)],
        out_specs=(spec(pl.ANY), spec(VMEM)),
        scratch_shapes=[VMEM((16, 2 * HEAD), BF16), pltpu.SemaphoreType.DMA((33,))],
        compiler_params=params,
        name="pack",
    )(where, table, held_pool, node, queries.reshape(2, HALF * 8, HEAD))
    peer = lax.ppermute(send, "core", [(0, 1), (1, 0)])

    every_query = lax.all_to_all(message, ("x", "y", "core"), 0, 0, tiled=True)

    own, pool_copy, mask = pl.pallas_call(
        prepare_kernel,
        out_shape=(
            shape((HALF * SPAN, 2 * HEAD), BF16),
            shape(pool.shape, pool.dtype),
            shape((HALF, 16, 2 * NODES), F32),
        ),
        in_specs=[spec(SMEM), spec(SMEM), spec(HBM), spec(VMEM)],
        out_specs=(spec(VMEM), spec(HBM), spec(VMEM)),
        scratch_shapes=[pltpu.SemaphoreType.DMA((33,))],
        compiler_params=params,
        cost_estimate=pl.CostEstimate(flops=50_000_000, bytes_accessed=7_000_000, transcendentals=0),
        name="prepare",
    )(where, table, held_pool, parents)
    mask, weight = lax.optimization_barrier((mask, out_weight))
    weights = [weight]
    for step in range(1, NEIGHBOURS):
        ring = [((i + step) % NEIGHBOURS, i) for i in range(NEIGHBOURS)]
        weights.append(lax.ppermute(weight, "x", ring))
    mask, *weights = lax.optimization_barrier((mask, *weights))

    partial = pl.pallas_call(
        attend_kernel,
        out_shape=shape((CHIPS, BLOCK, HEAD), BF16),
        in_specs=[spec(SMEM), spec(SMEM)] + [spec(VMEM)] * 5,
        out_specs=spec(VMEM),
        compiler_params=params,
        name="attend",
    )(where, lengths, every_query, own, peer, node, mask)

    parts = lax.all_to_all(partial, ("x", "y"), 0, 0, tiled=True)
    mixed = pl.pallas_call(
        combine_kernel,
        out_shape=shape((16, BLOCK, HEAD), BF16),
        in_specs=[spec(SMEM), spec(SMEM), spec(VMEM)],
        out_specs=spec(VMEM),
        compiler_params=params,
        name="combine",
    )(where, path, parts)
    attention = lax.all_to_all(mixed, ("y", "core"), 0, 0, tiled=True)

    sums = pl.pallas_call(
        project_kernel,
        out_shape=shape((32, 2, 8, HEAD), F32),
        in_specs=[spec(SMEM)] + [spec(VMEM)] * 5,
        out_specs=spec(VMEM),
        compiler_params=params,
        name="project",
    )(where, attention, *weights)
    shares = lax.all_to_all(sums, ("x", "tp"), 0, 0, tiled=True)
    projected = pl.pallas_call(
        sum_kernel,
        out_shape=shape((REQUESTS, 8, HEAD), F32),
        in_specs=[spec(VMEM)],
        out_specs=spec(VMEM),
        compiler_params=params,
        name="sum",
    )(shares)

    updated_pool, new_table = pl.pallas_call(
        write_kernel,
        out_shape=(shape(pool.shape, pool.dtype), shape(table.shape, table.dtype)),
        in_specs=[spec(SMEM)] * 5 + [spec(VMEM), spec(VMEM), spec(HBM)],
        out_specs=(spec(HBM), spec(SMEM)),
        input_output_aliases={7: 0},
        scratch_shapes=[VMEM((2 * REQUESTS, PAGE, 2 * HEAD), BF16), pltpu.SemaphoreType.DMA((2 * REQUESTS,))],
        compiler_params=params,
        name="write",
    )(where, table, lengths, counts, free_slot, table, attention, pool_copy)
    return projected, updated_pool, new_table


def solution(mesh):
    fine = Mesh(mesh.devices.reshape(4, 8, 2, 8), ("x", "y", "core", "tp"))
    ctx = ("x", "y", "core")
    placed = (
        P(None, ctx, "tp"),
        P(None, ctx, "tp"),
        P(ctx, None, "tp"),
        P("tp", ctx),
        P(),
        P(),
        P(),
        P(),
        P(None, ctx),
        P(None, ctx),
    )
    return jax.shard_map(
        on_device,
        mesh=fine,
        in_specs=placed,
        out_specs=(P(None, "tp", ctx), P(ctx, None, "tp"), P(None, ctx)),
        check_vma=False,
    )
```

```python
import jax
import jax.numpy as jnp
from jax import lax
from jax.experimental import pallas as pl
from jax.experimental.pallas import tpu as pltpu
from jax.sharding import Mesh, PartitionSpec as P

F32 = jnp.float32
BF16 = jnp.bfloat16

HEAD = 128
PATH_ROWS = 8
PAGE = 64
REQUESTS = 8
HALF = 4
NODES = 64
PAGES_LOCAL = 8
SPAN = PAGE * PAGES_LOCAL
LANES = 8 * NODES
CHIPS = 32
TAIL = 8
BLOCK = 64 + TAIL
NEIGHBOURS = 4
DEAD = -1e30
FLOOR = -1e28
LOG2E = 1.4426950408889634
SCALE2 = HEAD ** (-0.5) * LOG2E

NODE_ROWS0 = HALF * SPAN
SEND_ROWS = NODE_ROWS0 + 16

VMEM = pltpu.VMEM
SMEM = pltpu.SMEM
HBM = pltpu.HBM
LIMIT = 40 * 1024 * 1024


def iota(shape, dim):
    return lax.broadcasted_iota(jnp.int32, shape, dim)


def dot(a, b, ca=1, cb=0):
    return lax.dot_general(a, b, (((ca,), (cb,)), ((), ())), preferred_element_type=F32)


def ctx_index():
    return (lax.axis_index("x") * 8 + lax.axis_index("y")) * 2 + lax.axis_index("core")


def position():
    return lax.axis_index("core"), ctx_index()


def pack_kernel(table, pool, node, query, send, message, sems):
    other = HALF * (1 - lax.axis_index("core"))
    copies = []
    for r in range(HALF):
        for p in range(PAGES_LOCAL):
            n = r * PAGES_LOCAL + p
            copies.append(
                pltpu.make_async_copy(
                    pool.at[table[other + r, p]], send.at[pl.ds(n * PAGE, PAGE), :], sems.at[n]
                )
            )
    for c in copies:
        c.start()
    rows = node[...].astype(F32)
    send[pl.ds(NODE_ROWS0, 16), :] = jnp.concatenate([rows, jnp.zeros_like(rows)], axis=0).astype(BF16)
    flat = query[...].astype(F32)
    for half in range(2):
        rows = [
            flat[r : r + 1, h * HEAD : (h + 1) * HEAD] for r in range(HALF * half, HALF * half + HALF) for h in range(8)
        ]
        rows = jnp.concatenate(rows, axis=0).astype(BF16)
        for chip in range(CHIPS):
            message[2 * chip + half] = rows
    for c in copies:
        c.wait()


def prepare_kernel(table, pool, parents, own, pool_copy, mask, held, sems):
    core, ctx = position()
    copies = []
    for r in range(HALF):
        for p in range(PAGES_LOCAL):
            n = r * PAGES_LOCAL + p
            copies.append(
                pltpu.make_async_copy(
                    pool.at[table[HALF * core + r, p]], own.at[pl.ds(n * PAGE, PAGE), :], sems.at[n]
                )
            )
    fetch = pltpu.make_async_copy(pool, held, sems.at[32])
    fetch.start()
    for c in copies:
        c.start()
    up = iota((NODES, NODES), 0)
    down = iota((NODES, NODES), 1)
    twice = (iota((NODES, 2 * NODES), 0) == iota((NODES, 2 * NODES), 1) % NODES).astype(F32).astype(BF16)
    pick_row = iota((16, NODES), 0)
    pick_node = iota((16, NODES), 1)
    reach = []
    for r in range(HALF):
        link = parents[pl.ds(HALF * core + r, 1), :]
        reach.append(((up == link) | (up == down)).astype(F32).astype(BF16))
    for _ in range(6):
        reach = [jnp.minimum(dot(m, m), 1.0).astype(BF16) for m in reach]
    for r in range(HALF):
        mine = HALF * core + r
        pick = ((pick_row == mine) & (pick_node == ctx)) | (
            (pick_row == REQUESTS + mine) & (pick_node == ctx + 1 - 2 * core)
        )
        seen = dot(pick.astype(F32).astype(BF16), reach[r]).astype(BF16)
        mask[r] = dot(seen, twice)
    fetch.wait()
    store = pltpu.make_async_copy(held, pool_copy, sems.at[33])
    store.start()
    for c in copies:
        c.wait()
    store.wait()


def attend_kernel(lengths, queries, own, peer, node, mask, out):
    core, ctx = position()
    lane = iota((LANES, LANES), 1)
    order = (iota((LANES, LANES), 0) == (lane % NODES) * 8 + lane // NODES).astype(F32).astype(BF16)
    peer_node = peer[pl.ds(NODE_ROWS0, 16), :].astype(F32)[:REQUESTS]
    own_node = node[...].astype(F32)
    nodes = jnp.concatenate([own_node, peer_node], axis=0).astype(BF16)
    ones = jnp.ones((16, SPAN), BF16)
    ones_tree = jnp.ones((16, 16), BF16)
    row = iota((SPAN, LANES), 0)
    tail_row = iota((TAIL, HEAD), 0)
    for r in range(HALF):
        part = queries[:, pl.ds((r // 2) * 16, 16), :].astype(F32)[:, (r % 2) * 8 : (r % 2) * 8 + 8, :]
        part = part.reshape(LANES, HEAD).astype(BF16)
        query = dot(part, order, 0, 0).astype(BF16)
        length = lengths[HALF * core + r]
        span_own = own[pl.ds(r * SPAN, SPAN), :]
        span_peer = peer[pl.ds(r * SPAN, SPAN), :]
        live_own = row < length - ctx * SPAN
        live_peer = row < length - (ctx + 1 - 2 * core) * SPAN
        seen = jnp.concatenate([mask[r]] * 4, axis=1)
        s_own = jnp.where(live_own, dot(span_own[:, :HEAD], query), DEAD)
        s_peer = jnp.where(live_peer, dot(span_peer[:, :HEAD], query), DEAD)
        s_tree = jnp.where(seen > 0.5, dot(nodes[:, :HEAD], query), DEAD)
        peak = jnp.maximum(
            jnp.maximum(jnp.max(s_own, axis=0, keepdims=True), jnp.max(s_peer, axis=0, keepdims=True)),
            jnp.max(s_tree, axis=0, keepdims=True),
        )
        peak = jnp.maximum(peak, FLOOR) * SCALE2
        total = None
        for s, v, one in (
            (s_own, span_own[:, HEAD:], ones),
            (s_peer, span_peer[:, HEAD:], ones),
            (s_tree, nodes[:, HEAD:], ones_tree),
        ):
            p = jnp.exp2(s * SCALE2 - peak)
            lhs = jnp.concatenate([v.astype(F32).T.astype(BF16), one], axis=0)
            high = p.astype(BF16)
            low = (p - high.astype(F32)).astype(BF16)
            add = dot(lhs, high) + dot(lhs, low)
            total = add if total is None else total + add
        row_sum = total[HEAD : HEAD + 1]
        some = row_sum > 0.0
        mixed = total[:HEAD] * (1.0 / jnp.where(some, row_sum, 1.0))
        log_sum = jnp.where(some, peak + jnp.log2(jnp.where(some, row_sum, 1.0)), DEAD)
        first = log_sum.astype(BF16).astype(F32)
        rest = log_sum - first
        second = rest.astype(BF16).astype(F32)
        third = rest - second
        for y in range(8):
            lanes = slice((y // 2) * HEAD, (y // 2 + 1) * HEAD)
            half = y % 2
            terms = (
                first[:, lanes],
                second[:, lanes],
                third[:, lanes],
                own_node[y : y + 1, :HEAD],
                own_node[y : y + 1, HEAD:],
                peer_node[y : y + 1, :HEAD],
                peer_node[y : y + 1, HEAD:],
            )
            tail = jnp.zeros((TAIL, HEAD), F32)
            for t, term in enumerate(terms):
                tail = jnp.where(tail_row == t, term, tail)
            block = jnp.concatenate([mixed[half * 64 : half * 64 + 64, lanes], tail], axis=0)
            out[r * 8 + y] = block.astype(BF16)


def combine_kernel(path, got, out):
    core = lax.axis_index("core")
    y = lax.axis_index("y")
    logs = []
    for s in range(CHIPS):
        tail = got[s].astype(F32)[64:BLOCK]
        logs.append(tail[0:1] + tail[1:2] + tail[2:3])
    peak = logs[0]
    for s in range(1, CHIPS):
        peak = jnp.maximum(peak, logs[s])
    total = jnp.zeros((1, HEAD), F32)
    mixed = jnp.zeros((64, HEAD), F32)
    for s in range(CHIPS):
        share = jnp.exp2(logs[s] - peak)
        total = total + share
        mixed = mixed + share * got[s].astype(F32)[:64]
    mixed = mixed * (1.0 / total)
    tail_row = iota((TAIL, HEAD), 0)
    tail = jnp.zeros((TAIL, HEAD), F32)
    for j in range(HALF):
        node = path[y, HALF * core + j]
        held = got[node // 2].astype(F32)[64:BLOCK]
        is_own = node % 2 == core
        key = jnp.where(is_own, held[3:4], held[5:6])
        value = jnp.where(is_own, held[4:5], held[6:7])
        tail = jnp.where(tail_row == 2 * j, key, tail)
        tail = jnp.where(tail_row == 2 * j + 1, value, tail)
    block = jnp.concatenate([mixed, tail], axis=0).astype(BF16)
    for s in range(16):
        out[s] = block


def project_kernel(got, w0, w1, w2, w3, out):
    x = lax.axis_index("x")
    held = got[...].reshape(8, 2, BLOCK, HEAD)
    weights = (w0, w1, w2, w3)
    for pair in range(NEIGHBOURS // 2):
        wide = []
        for h in range(2):
            cols = []
            for n in (2 * pair, 2 * pair + 1):
                rows = [weights[n][(2 * p + h) * HEAD : (2 * p + h + 1) * HEAD, :] for p in range(4)]
                cols.append(jnp.concatenate(rows, axis=0))
            wide.append(jnp.concatenate(cols, axis=1))
        for k in range(2):
            a = held[:, k, :64, :].reshape(LANES, HEAD)
            sums = dot(a, wide[0], 0, 0)[:NODES] + dot(a, wide[1], 0, 0)[NODES:]
            for n in range(2):
                to = lax.rem(x + 2 * pair + n, NEIGHBOURS)
                for t in range(8):
                    out[to * 8 + t, k] = sums[t * 8 : t * 8 + 8, n * HEAD : (n + 1) * HEAD]


def sum_kernel(got, out):
    for x in range(NEIGHBOURS):
        total = got[x * 8]
        for t in range(1, 8):
            total = total + got[x * 8 + t]
        out[x] = total[0]
        out[HALF + x] = total[1]


def write_kernel(table, lengths, counts, spare, table_v, got, pool_in, pool, new_table, pages, sems):
    ctx = ctx_index()
    for r in range(REQUESTS):
        for p in range(PAGES_LOCAL):
            new_table[r, p] = table[r, p]
    row = iota((PAGE, 2 * HEAD), 0)
    for r in range(REQUESTS):
        length = lengths[r]
        count = counts[r]
        tail_page = length // PAGE
        for step in range(2):
            page = tail_page + step
            local = page - ctx * PAGES_LOCAL
            first = length - page * PAGE
            here = (local >= 0) & (local < PAGES_LOCAL)
            if step == 1:
                here = here & (first + count > 0)

            @pl.when(here)
            def _():
                slot = table[r, local]
                target = slot
                if step == 0:
                    uses = jnp.sum((table_v[...] == slot).astype(jnp.int32))
                    target = jnp.where(uses > 1, spare[r, 0], slot)
                    new_table[r, local] = target
                fetch = pltpu.make_async_copy(pool_in.at[slot], pages.at[2 * r + step], sems.at[2 * r + step])
                fetch.start()
                fetch.wait()
                now = pages[2 * r + step].astype(F32)
                for j in range(PATH_ROWS):
                    held = got[2 * r + j // HALF].astype(F32)[64:BLOCK]
                    at = 2 * (j % HALF)
                    new = jnp.concatenate([held[at : at + 1], held[at + 1 : at + 2]], axis=1)
                    now = jnp.where((row == first + j) & (j < count), new, now)
                pages[2 * r + step] = now.astype(BF16)
                store = pltpu.make_async_copy(pages.at[2 * r + step], pool.at[target], sems.at[2 * r + step])
                store.start()
                store.wait()


def spec(space):
    return pl.BlockSpec(memory_space=space)


def on_device(queries, node_kv, pool, out_weight, parents, path, counts, lengths, table, free_slot):
    params = pltpu.CompilerParams(vmem_limit_bytes=LIMIT)
    shape = jax.ShapeDtypeStruct
    node = node_kv.reshape(REQUESTS, 2 * HEAD)
    held_pool, held_table, held_node, held_queries = (
        pltpu.with_memory_space_constraint(a, HBM)
        for a in (pool, table, node, queries.reshape(REQUESTS, 8 * HEAD))
    )

    send, message = pl.pallas_call(
        pack_kernel,
        out_shape=(VMEM((SEND_ROWS, 2 * HEAD), BF16), VMEM((2 * CHIPS, HALF * 8, HEAD), BF16)),
        in_specs=[spec(SMEM), spec(HBM), spec(VMEM), spec(VMEM)],
        out_specs=(spec(VMEM), spec(VMEM)),
        scratch_shapes=[pltpu.SemaphoreType.DMA((32,))],
        compiler_params=params,
        name="pack",
    )(held_table, held_pool, held_node, held_queries)
    peer = lax.ppermute(send, "core", [(0, 1), (1, 0)])

    every_query = lax.all_to_all(message, ("x", "y", "core"), 0, 0, tiled=True)

    own, pool_copy, mask = pl.pallas_call(
        prepare_kernel,
        out_shape=(
            shape((HALF * SPAN, 2 * HEAD), BF16),
            shape(pool.shape, pool.dtype),
            shape((HALF, 16, 2 * NODES), F32),
        ),
        in_specs=[spec(SMEM), spec(HBM), spec(VMEM)],
        out_specs=(spec(VMEM), spec(HBM), spec(VMEM)),
        scratch_shapes=[VMEM(pool.shape, BF16), pltpu.SemaphoreType.DMA((34,))],
        compiler_params=params,
        cost_estimate=pl.CostEstimate(flops=50_000_000, bytes_accessed=7_000_000, transcendentals=0),
        name="prepare",
    )(table, held_pool, parents)

    partial = pl.pallas_call(
        attend_kernel,
        out_shape=shape((CHIPS, BLOCK, HEAD), BF16),
        in_specs=[spec(SMEM)] + [spec(VMEM)] * 5,
        out_specs=spec(VMEM),
        compiler_params=params,
        name="attend",
    )(lengths, every_query, own, peer, node, mask)

    partial, weight = lax.optimization_barrier((partial, out_weight))
    weights = [weight]
    for step in range(1, NEIGHBOURS):
        ring = [((i + step) % NEIGHBOURS, i) for i in range(NEIGHBOURS)]
        weights.append(lax.ppermute(weight, "x", ring))
    parts = lax.all_to_all(partial, ("x", "y"), 0, 0, tiled=True)
    parts, *weights = lax.optimization_barrier((parts, *weights))
    mixed = pl.pallas_call(
        combine_kernel,
        out_shape=shape((16, BLOCK, HEAD), BF16),
        in_specs=[spec(SMEM), spec(VMEM)],
        out_specs=spec(VMEM),
        compiler_params=params,
        name="combine",
    )(path, parts)
    attention = lax.all_to_all(mixed, ("y", "core"), 0, 0, tiled=True)

    sums = pl.pallas_call(
        project_kernel,
        out_shape=shape((32, 2, 8, HEAD), F32),
        in_specs=[spec(VMEM)] * 5,
        out_specs=spec(VMEM),
        compiler_params=params,
        name="project",
    )(attention, *weights)
    shares = lax.all_to_all(sums, ("x", "tp"), 0, 0, tiled=True)
    projected = pl.pallas_call(
        sum_kernel,
        out_shape=shape((REQUESTS, 8, HEAD), F32),
        in_specs=[spec(VMEM)],
        out_specs=spec(VMEM),
        compiler_params=params,
        name="sum",
    )(shares)

    updated_pool, new_table = pl.pallas_call(
        write_kernel,
        out_shape=(shape(pool.shape, pool.dtype), shape(table.shape, table.dtype)),
        in_specs=[spec(SMEM)] * 4 + [spec(VMEM), spec(VMEM), spec(HBM)],
        out_specs=(spec(HBM), spec(SMEM)),
        input_output_aliases={6: 0},
        scratch_shapes=[VMEM((2 * REQUESTS, PAGE, 2 * HEAD), BF16), pltpu.SemaphoreType.DMA((2 * REQUESTS,))],
        compiler_params=params,
        name="write",
    )(table, lengths, counts, free_slot, table, attention, pool_copy)
    return projected, updated_pool, new_table


def solution(mesh):
    fine = Mesh(mesh.devices.reshape(4, 8, 2, 8), ("x", "y", "core", "tp"))
    ctx = ("x", "y", "core")
    placed = (
        P(None, ctx, "tp"),
        P(None, ctx, "tp"),
        P(ctx, None, "tp"),
        P("tp", ctx),
        P(),
        P(),
        P(),
        P(),
        P(None, ctx),
        P(None, ctx),
    )
    return jax.shard_map(
        on_device,
        mesh=fine,
        in_specs=placed,
        out_specs=(P(None, "tp", ctx), P(ctx, None, "tp"), P(None, ctx)),
        check_vma=False,
    )
```

```python
import jax
import jax.numpy as jnp
from jax import lax
from jax.experimental import pallas as pl
from jax.experimental.pallas import tpu as pltpu
from jax.sharding import Mesh, PartitionSpec as P

F32 = jnp.float32
BF16 = jnp.bfloat16

HEAD = 128
PATH_ROWS = 8
PAGE = 64
REQUESTS = 8
HALF = 4
NODES = 64
PAGES_LOCAL = 8
SPAN = PAGE * PAGES_LOCAL
LANES = 8 * NODES
CHIPS = 32
TAIL = 8
BLOCK = 64 + TAIL
DEAD = -1e30
FLOOR = -1e28
LOG2E = 1.4426950408889634
SCALE2 = HEAD ** (-0.5) * LOG2E

SENDS = 2
EACH = HALF // SENDS
NODE_ROWS0 = EACH * SPAN
W_ROWS = 512

VMEM = pltpu.VMEM
SMEM = pltpu.SMEM
HBM = pltpu.HBM
LIMIT = 40 * 1024 * 1024


def iota(shape, dim):
    return lax.broadcasted_iota(jnp.int32, shape, dim)


def dot(a, b, ca=1, cb=0):
    return lax.dot_general(a, b, (((ca,), (cb,)), ((), ())), preferred_element_type=F32)


def ctx_index():
    return (lax.axis_index("x") * 8 + lax.axis_index("y")) * 2 + lax.axis_index("core")


def position():
    return lax.axis_index("core"), ctx_index()


def message_kernel(query, message):
    flat = query[...].astype(F32)
    for half in range(2):
        rows = [
            flat[r : r + 1, h * HEAD : (h + 1) * HEAD] for r in range(HALF * half, HALF * half + HALF) for h in range(8)
        ]
        rows = jnp.concatenate(rows, axis=0).astype(BF16)
        for chip in range(CHIPS):
            message[2 * chip + half] = rows


def prepare_kernel(table, pool, node, parents, weight, send0, send1, own, pool_copy, mask, held, sems):
    core, ctx = position()
    copies = []
    sends = (send0, send1)
    for mine in range(2):
        for r in range(HALF):
            for p in range(PAGES_LOCAL):
                slot = table[HALF * (core if mine else 1 - core) + r, p]
                to, n = (own, r * PAGES_LOCAL + p) if mine else (sends[r // EACH], (r % EACH) * PAGES_LOCAL + p)
                if not mine and r >= EACH:
                    n += PAGES_LOCAL
                at = mine * 32 + r * PAGES_LOCAL + p
                copies.append(pltpu.make_async_copy(pool.at[slot], to.at[pl.ds(n * PAGE, PAGE), :], sems.at[at]))
    for half in range(2):
        copies.append(
            pltpu.make_async_copy(
                weight.at[pl.ds(half * W_ROWS, W_ROWS), :],
                send1.at[pl.ds(0, W_ROWS), pl.ds(half * HEAD, HEAD)],
                sems.at[66 + half],
            )
        )
    fetch = pltpu.make_async_copy(pool, held, sems.at[64])
    for c in copies:
        c.start()
    fetch.start()
    rows = node[...].astype(F32)
    send0[pl.ds(NODE_ROWS0, 16), :] = jnp.concatenate([rows, jnp.zeros_like(rows)], axis=0).astype(BF16)
    up = iota((NODES, NODES), 0)
    down = iota((NODES, NODES), 1)
    twice = (iota((NODES, 2 * NODES), 0) == iota((NODES, 2 * NODES), 1) % NODES).astype(F32).astype(BF16)
    pick_row = iota((16, NODES), 0)
    pick_node = iota((16, NODES), 1)
    reach = []
    for r in range(HALF):
        link = parents[pl.ds(HALF * core + r, 1), :]
        reach.append(((up == link) | (up == down)).astype(F32).astype(BF16))
    for _ in range(6):
        reach = [jnp.minimum(dot(m, m), 1.0).astype(BF16) for m in reach]
    for r in range(HALF):
        mine = HALF * core + r
        pick = ((pick_row == mine) & (pick_node == ctx)) | (
            (pick_row == REQUESTS + mine) & (pick_node == ctx + 1 - 2 * core)
        )
        seen = dot(pick.astype(F32).astype(BF16), reach[r]).astype(BF16)
        mask[r] = dot(seen, twice)
    fetch.wait()
    store = pltpu.make_async_copy(held, pool_copy, sems.at[65])
    store.start()
    for c in copies:
        c.wait()
    store.wait()


def attend_kernel(lengths, queries, own, node, mask, peer0, peer1, out):
    core, ctx = position()
    lane = iota((LANES, LANES), 1)
    order = (iota((LANES, LANES), 0) == (lane % NODES) * 8 + lane // NODES).astype(F32).astype(BF16)
    peers = (peer0, peer1)
    peer_node = peer0[pl.ds(NODE_ROWS0, 16), :].astype(F32)[:REQUESTS]
    own_node = node[...].astype(F32)
    nodes = jnp.concatenate([own_node, peer_node], axis=0).astype(BF16)
    ones = jnp.ones((16, SPAN), BF16)
    ones_tree = jnp.ones((16, 16), BF16)
    row = iota((SPAN, LANES), 0)
    tail_row = iota((TAIL, HEAD), 0)
    for r in range(HALF):
        part = queries[:, pl.ds((r // 2) * 16, 16), :].astype(F32)[:, (r % 2) * 8 : (r % 2) * 8 + 8, :]
        part = part.reshape(LANES, HEAD).astype(BF16)
        query = dot(part, order, 0, 0).astype(BF16)
        length = lengths[HALF * core + r]
        span_own = own[pl.ds(r * SPAN, SPAN), :]
        span_peer = peers[r // EACH][pl.ds((r // EACH + r % EACH) * SPAN, SPAN), :]
        live_own = row < length - ctx * SPAN
        live_peer = row < length - (ctx + 1 - 2 * core) * SPAN
        seen = jnp.concatenate([mask[r]] * 4, axis=1)
        s_own = jnp.where(live_own, dot(span_own[:, :HEAD], query), DEAD)
        s_peer = jnp.where(live_peer, dot(span_peer[:, :HEAD], query), DEAD)
        s_tree = jnp.where(seen > 0.5, dot(nodes[:, :HEAD], query), DEAD)
        peak = jnp.maximum(
            jnp.maximum(jnp.max(s_own, axis=0, keepdims=True), jnp.max(s_peer, axis=0, keepdims=True)),
            jnp.max(s_tree, axis=0, keepdims=True),
        )
        peak = jnp.maximum(peak, FLOOR) * SCALE2
        total = None
        for s, v, one in (
            (s_own, span_own[:, HEAD:], ones),
            (s_peer, span_peer[:, HEAD:], ones),
            (s_tree, nodes[:, HEAD:], ones_tree),
        ):
            p = jnp.exp2(s * SCALE2 - peak)
            lhs = jnp.concatenate([v.astype(F32).T.astype(BF16), one], axis=0)
            high = p.astype(BF16)
            low = (p - high.astype(F32)).astype(BF16)
            add = dot(lhs, high) + dot(lhs, low)
            total = add if total is None else total + add
        row_sum = total[HEAD : HEAD + 1]
        some = row_sum > 0.0
        mixed = total[:HEAD] * (1.0 / jnp.where(some, row_sum, 1.0))
        log_sum = jnp.where(some, peak + jnp.log2(jnp.where(some, row_sum, 1.0)), DEAD)
        first = log_sum.astype(BF16).astype(F32)
        rest = log_sum - first
        second = rest.astype(BF16).astype(F32)
        third = rest - second
        for y in range(8):
            lanes = slice((y // 2) * HEAD, (y // 2 + 1) * HEAD)
            half = y % 2
            terms = (
                first[:, lanes],
                second[:, lanes],
                third[:, lanes],
                own_node[y : y + 1, :HEAD],
                own_node[y : y + 1, HEAD:],
                peer_node[y : y + 1, :HEAD],
                peer_node[y : y + 1, HEAD:],
            )
            tail = jnp.zeros((TAIL, HEAD), F32)
            for t, term in enumerate(terms):
                tail = jnp.where(tail_row == t, term, tail)
            block = jnp.concatenate([mixed[half * 64 : half * 64 + 64, lanes], tail], axis=0)
            out[r * 8 + y] = block.astype(BF16)


def combine_kernel(path, got, out):
    core = lax.axis_index("core")
    x = lax.axis_index("x")
    y = lax.axis_index("y")
    logs = []
    for s in range(CHIPS):
        tail = got[s].astype(F32)[64:BLOCK]
        logs.append(tail[0:1] + tail[1:2] + tail[2:3])
    peak = logs[0]
    for s in range(1, CHIPS):
        peak = jnp.maximum(peak, logs[s])
    total = jnp.zeros((1, HEAD), F32)
    mixed = jnp.zeros((64, HEAD), F32)
    for s in range(CHIPS):
        share = jnp.exp2(logs[s] - peak)
        total = total + share
        mixed = mixed + share * got[s].astype(F32)[:64]
    mixed = mixed * (1.0 / total)
    tail_row = iota((TAIL, HEAD), 0)
    tail = jnp.zeros((TAIL, HEAD), F32)
    for j in range(2):
        node = path[y, 2 * x + j]
        held = got[node // 2].astype(F32)[64:BLOCK]
        is_own = node % 2 == core
        key = jnp.where(is_own, held[3:4], held[5:6])
        value = jnp.where(is_own, held[4:5], held[6:7])
        tail = jnp.where(tail_row == 2 * j, key, tail)
        tail = jnp.where(tail_row == 2 * j + 1, value, tail)
    block = jnp.concatenate([mixed, tail], axis=0).astype(BF16)
    for s in range(CHIPS):
        out[s] = block


def project_kernel(got, weight, peer, out):
    core = lax.axis_index("core")
    sides = []
    for h in range(2):
        own_h = [weight[(2 * p + h) * HEAD : (2 * p + h + 1) * HEAD, :] for p in range(4)]
        peer_h = []
        for p in range(4):
            at = (2 * p + h) * HEAD
            side = at // W_ROWS * HEAD
            peer_h.append(peer[at % W_ROWS : at % W_ROWS + HEAD, side : side + HEAD])
        sides.append(jnp.concatenate([jnp.concatenate(own_h, axis=0), jnp.concatenate(peer_h, axis=0)], axis=1))
    for r in range(HALF):
        a = got[pl.ds(r * 8, 8)][:, :64, :].reshape(LANES, HEAD)
        sums = dot(a, sides[0], 0, 0)[:NODES] + dot(a, sides[1], 0, 0)[NODES:]
        for t in range(8):
            rows = sums[t * 8 : t * 8 + 8]
            out[core * 8 + t, r] = rows[:, :HEAD]
            out[(1 - core) * 8 + t, r] = rows[:, HEAD:]


def sum_kernel(got, out):
    for core in range(2):
        total = got[core * 8]
        for t in range(1, 8):
            total = total + got[core * 8 + t]
        out[HALF * core : HALF * core + HALF] = total


def write_kernel(table, lengths, counts, spare, table_v, got, pool_in, pool, new_table, pages, sems):
    ctx = ctx_index()
    for r in range(REQUESTS):
        for p in range(PAGES_LOCAL):
            new_table[r, p] = table[r, p]
    row = iota((PAGE, 2 * HEAD), 0)
    for r in range(REQUESTS):
        length = lengths[r]
        count = counts[r]
        tail_page = length // PAGE
        for step in range(2):
            page = tail_page + step
            local = page - ctx * PAGES_LOCAL
            first = length - page * PAGE
            here = (local >= 0) & (local < PAGES_LOCAL)
            if step == 1:
                here = here & (first + count > 0)

            @pl.when(here)
            def _():
                slot = table[r, local]
                target = slot
                if step == 0:
                    uses = jnp.sum((table_v[...] == slot).astype(jnp.int32))
                    target = jnp.where(uses > 1, spare[r, 0], slot)
                    new_table[r, local] = target
                fetch = pltpu.make_async_copy(pool_in.at[slot], pages.at[2 * r + step], sems.at[2 * r + step])
                fetch.start()
                fetch.wait()
                now = pages[2 * r + step].astype(F32)
                for j in range(PATH_ROWS):
                    held = got[(j // 2) * 8 + r].astype(F32)[64:BLOCK]
                    at = 2 * (j % 2)
                    new = jnp.concatenate([held[at : at + 1], held[at + 1 : at + 2]], axis=1)
                    now = jnp.where((row == first + j) & (j < count), new, now)
                pages[2 * r + step] = now.astype(BF16)
                store = pltpu.make_async_copy(pages.at[2 * r + step], pool.at[target], sems.at[2 * r + step])
                store.start()
                store.wait()


def spec(space):
    return pl.BlockSpec(memory_space=space)


def on_device(queries, node_kv, pool, out_weight, parents, path, counts, lengths, table, free_slot):
    params = pltpu.CompilerParams(vmem_limit_bytes=LIMIT)
    shape = jax.ShapeDtypeStruct
    node = node_kv.reshape(REQUESTS, 2 * HEAD)
    held_pool, held_table, held_node, held_parents, held_weight, held_queries = (
        pltpu.with_memory_space_constraint(a, HBM)
        for a in (pool, table, node, parents, out_weight, queries.reshape(REQUESTS, 8 * HEAD))
    )

    message = pl.pallas_call(
        message_kernel,
        out_shape=shape((2 * CHIPS, HALF * 8, HEAD), BF16),
        in_specs=[spec(VMEM)],
        out_specs=spec(VMEM),
        compiler_params=params,
        name="message",
    )(held_queries)
    every_query = lax.all_to_all(message, ("x", "y", "core"), 0, 0, tiled=True)

    *sends, own, pool_copy, mask = pl.pallas_call(
        prepare_kernel,
        out_shape=(
            *(shape((NODE_ROWS0 + extra, 2 * HEAD), BF16) for extra in (16, W_ROWS)),
            shape((HALF * SPAN, 2 * HEAD), BF16),
            shape(pool.shape, pool.dtype),
            shape((HALF, 16, 2 * NODES), F32),
        ),
        in_specs=[spec(SMEM), spec(HBM), spec(VMEM), spec(VMEM), spec(HBM)],
        out_specs=(*([spec(VMEM)] * (SENDS + 1)), spec(HBM), spec(VMEM)),
        scratch_shapes=[VMEM(pool.shape, BF16), pltpu.SemaphoreType.DMA((68,))],
        compiler_params=params,
        cost_estimate=pl.CostEstimate(flops=50_000_000, bytes_accessed=7_000_000, transcendentals=0),
        name="prepare",
    )(held_table, held_pool, held_node, held_parents, held_weight)
    peers = [lax.ppermute(a, "core", [(0, 1), (1, 0)]) for a in sends]
    mask, *peers = lax.optimization_barrier((mask, *peers))

    partial = pl.pallas_call(
        attend_kernel,
        out_shape=shape((CHIPS, BLOCK, HEAD), BF16),
        in_specs=[spec(SMEM)] + [spec(VMEM)] * (4 + SENDS),
        out_specs=spec(VMEM),
        compiler_params=params,
        name="attend",
    )(lengths, every_query, own, node, mask, *peers)

    parts = lax.all_to_all(partial, ("x", "y"), 0, 0, tiled=True)
    mixed = pl.pallas_call(
        combine_kernel,
        out_shape=shape((CHIPS, BLOCK, HEAD), BF16),
        in_specs=[spec(SMEM), spec(VMEM)],
        out_specs=spec(VMEM),
        compiler_params=params,
        name="combine",
    )(path, parts)
    attention = lax.all_to_all(mixed, ("x", "y"), 0, 0, tiled=True)

    sums = pl.pallas_call(
        project_kernel,
        grid=(1,),
        out_shape=shape((16, HALF, 8, HEAD), F32),
        in_specs=[
            pl.BlockSpec((CHIPS, BLOCK, HEAD), lambda i: (0, 0, 0)),
            pl.BlockSpec((8 * HEAD, HEAD), lambda i: (0, 0)),
            pl.BlockSpec((W_ROWS, 2 * HEAD), lambda i: (0, 0)),
        ],
        out_specs=pl.BlockSpec((16, HALF, 8, HEAD), lambda i: (0, 0, 0, 0)),
        compiler_params=params,
        name="project",
    )(attention, out_weight, peers[1])
    shares = lax.all_to_all(sums, ("core", "tp"), 0, 0, tiled=True)
    projected = pl.pallas_call(
        sum_kernel,
        out_shape=shape((REQUESTS, 8, HEAD), F32),
        in_specs=[spec(VMEM)],
        out_specs=spec(VMEM),
        compiler_params=params,
        name="sum",
    )(shares)

    updated_pool, new_table = pl.pallas_call(
        write_kernel,
        out_shape=(shape(pool.shape, pool.dtype), shape(table.shape, table.dtype)),
        in_specs=[spec(SMEM)] * 4 + [spec(VMEM), spec(VMEM), spec(HBM)],
        out_specs=(spec(HBM), spec(SMEM)),
        input_output_aliases={6: 0},
        scratch_shapes=[VMEM((2 * REQUESTS, PAGE, 2 * HEAD), BF16), pltpu.SemaphoreType.DMA((2 * REQUESTS,))],
        compiler_params=params,
        name="write",
    )(table, lengths, counts, free_slot, table, attention, pool_copy)
    return projected, updated_pool, new_table


def solution(mesh):
    fine = Mesh(mesh.devices.reshape(4, 8, 2, 8), ("x", "y", "core", "tp"))
    ctx = ("x", "y", "core")
    placed = (
        P(None, ctx, "tp"),
        P(None, ctx, "tp"),
        P(ctx, None, "tp"),
        P("tp", ctx),
        P(),
        P(),
        P(),
        P(),
        P(None, ctx),
        P(None, ctx),
    )
    return jax.shard_map(
        on_device,
        mesh=fine,
        in_specs=placed,
        out_specs=(P(None, "tp", ctx), P(ctx, None, "tp"), P(None, ctx)),
        check_vma=False,
    )
```

```python
import jax
import jax.numpy as jnp
from jax import lax
from jax.experimental import pallas as pl
from jax.experimental.pallas import tpu as pltpu
from jax.sharding import Mesh, PartitionSpec as P

F32 = jnp.float32
BF16 = jnp.bfloat16

HEAD = 128
PATH_ROWS = 8
PAGE = 64
REQUESTS = 8
HALF = 4
NODES = 64
PAGES_LOCAL = 8
SPAN = PAGE * PAGES_LOCAL
LANES = 8 * NODES
CHIPS = 32
TAIL = 8
BLOCK = 64 + TAIL
DEAD = -1e30
FLOOR = -1e28
LOG2E = 1.4426950408889634
SCALE2 = HEAD ** (-0.5) * LOG2E

SENDS = 2
EACH = HALF // SENDS
NODE_ROWS0 = EACH * SPAN
W_ROWS = 512

VMEM = pltpu.VMEM
SMEM = pltpu.SMEM
HBM = pltpu.HBM
LIMIT = 40 * 1024 * 1024


def iota(shape, dim):
    return lax.broadcasted_iota(jnp.int32, shape, dim)


def dot(a, b, ca=1, cb=0):
    return lax.dot_general(a, b, (((ca,), (cb,)), ((), ())), preferred_element_type=F32)


def ctx_index():
    return (lax.axis_index("x") * 8 + lax.axis_index("y")) * 2 + lax.axis_index("core")


def position():
    return lax.axis_index("core"), ctx_index()


def message_kernel(query, message):
    flat = query[...].astype(F32)
    for half in range(2):
        rows = [
            flat[r : r + 1, h * HEAD : (h + 1) * HEAD] for r in range(HALF * half, HALF * half + HALF) for h in range(8)
        ]
        rows = jnp.concatenate(rows, axis=0).astype(BF16)
        for chip in range(CHIPS):
            message[2 * chip + half] = rows


def prepare_kernel(table, pool, node, parents, weight, send0, send1, own, pool_copy, mask, held, sems):
    core, ctx = position()
    copies = []
    sends = (send0, send1)
    for mine in range(2):
        for r in range(HALF):
            for p in range(PAGES_LOCAL):
                slot = table[HALF * (core if mine else 1 - core) + r, p]
                to, n = (own, r * PAGES_LOCAL + p) if mine else (sends[r // EACH], (r % EACH) * PAGES_LOCAL + p)
                if not mine and r >= EACH:
                    n += PAGES_LOCAL
                at = mine * 32 + r * PAGES_LOCAL + p
                copies.append(pltpu.make_async_copy(pool.at[slot], to.at[pl.ds(n * PAGE, PAGE), :], sems.at[at]))
    for half in range(2):
        copies.append(
            pltpu.make_async_copy(
                weight.at[pl.ds(half * W_ROWS, W_ROWS), :],
                send1.at[pl.ds(0, W_ROWS), pl.ds(half * HEAD, HEAD)],
                sems.at[66 + half],
            )
        )
    fetch = pltpu.make_async_copy(pool, held, sems.at[64])
    for c in copies:
        c.start()
    fetch.start()
    rows = node[...].astype(F32)
    send0[pl.ds(NODE_ROWS0, 16), :] = jnp.concatenate([rows, jnp.zeros_like(rows)], axis=0).astype(BF16)
    up = iota((NODES, NODES), 0)
    down = iota((NODES, NODES), 1)
    twice = (iota((NODES, 2 * NODES), 0) == iota((NODES, 2 * NODES), 1) % NODES).astype(F32).astype(BF16)
    pick_row = iota((16, NODES), 0)
    pick_node = iota((16, NODES), 1)
    reach = []
    for r in range(HALF):
        link = parents[pl.ds(HALF * core + r, 1), :]
        reach.append(((up == link) | (up == down)).astype(F32).astype(BF16))
    for step in range(6):
        reach = [jnp.minimum(dot(m, m), 1.0).astype(BF16) for m in reach]
        if step == 2:
            fetch.wait()
            store = pltpu.make_async_copy(held, pool_copy, sems.at[65])
            store.start()
    for r in range(HALF):
        mine = HALF * core + r
        pick = ((pick_row == mine) & (pick_node == ctx)) | (
            (pick_row == REQUESTS + mine) & (pick_node == ctx + 1 - 2 * core)
        )
        seen = dot(pick.astype(F32).astype(BF16), reach[r]).astype(BF16)
        mask[r] = dot(seen, twice)
    for c in copies:
        c.wait()
    store.wait()


def attend_kernel(lengths, queries, own, node, mask, peer0, peer1, out):
    core, ctx = position()
    lane = iota((LANES, LANES), 1)
    order = (iota((LANES, LANES), 0) == (lane % NODES) * 8 + lane // NODES).astype(F32).astype(BF16)
    peers = (peer0, peer1)
    peer_node = peer0[pl.ds(NODE_ROWS0, 16), :].astype(F32)[:REQUESTS]
    own_node = node[...].astype(F32)
    nodes = jnp.concatenate([own_node, peer_node], axis=0).astype(BF16)
    ones = jnp.ones((16, SPAN), BF16)
    ones_tree = jnp.ones((16, 16), BF16)
    row = iota((SPAN, LANES), 0)
    tail_row = iota((TAIL, HEAD), 0)
    def scores(r):
        part = queries[:, pl.ds((r // 2) * 16, 16), :].astype(F32)[:, (r % 2) * 8 : (r % 2) * 8 + 8, :]
        part = part.reshape(LANES, HEAD).astype(BF16)
        query = dot(part, order, 0, 0).astype(BF16)
        length = lengths[HALF * core + r]
        span_own = own[pl.ds(r * SPAN, SPAN), :]
        span_peer = peers[r // EACH][pl.ds((r // EACH + r % EACH) * SPAN, SPAN), :]
        live_own = row < length - ctx * SPAN
        live_peer = row < length - (ctx + 1 - 2 * core) * SPAN
        seen = jnp.concatenate([mask[r]] * 4, axis=1)
        s_own = jnp.where(live_own, dot(span_own[:, :HEAD], query), DEAD)
        s_peer = jnp.where(live_peer, dot(span_peer[:, :HEAD], query), DEAD)
        s_tree = jnp.where(seen > 0.5, dot(nodes[:, :HEAD], query), DEAD)
        peak = jnp.maximum(
            jnp.maximum(jnp.max(s_own, axis=0, keepdims=True), jnp.max(s_peer, axis=0, keepdims=True)),
            jnp.max(s_tree, axis=0, keepdims=True),
        )
        peak = jnp.maximum(peak, FLOOR) * SCALE2
        return s_own, s_peer, s_tree, span_own, span_peer, peak

    ahead = scores(0)
    for r in range(HALF):
        s_own, s_peer, s_tree, span_own, span_peer, peak = ahead
        if r + 1 < HALF:
            ahead = scores(r + 1)
        total = None
        for s, v, one in (
            (s_own, span_own[:, HEAD:], ones),
            (s_peer, span_peer[:, HEAD:], ones),
            (s_tree, nodes[:, HEAD:], ones_tree),
        ):
            p = jnp.exp2(s * SCALE2 - peak)
            lhs = jnp.concatenate([v.astype(F32).T.astype(BF16), one], axis=0)
            high = p.astype(BF16)
            low = (p - high.astype(F32)).astype(BF16)
            add = dot(lhs, high) + dot(lhs, low)
            total = add if total is None else total + add
        row_sum = total[HEAD : HEAD + 1]
        some = row_sum > 0.0
        mixed = total[:HEAD] * (1.0 / jnp.where(some, row_sum, 1.0))
        log_sum = jnp.where(some, peak + jnp.log2(jnp.where(some, row_sum, 1.0)), DEAD)
        first = log_sum.astype(BF16).astype(F32)
        rest = log_sum - first
        second = rest.astype(BF16).astype(F32)
        third = rest - second
        for y in range(8):
            lanes = slice((y // 2) * HEAD, (y // 2 + 1) * HEAD)
            half = y % 2
            terms = (
                first[:, lanes],
                second[:, lanes],
                third[:, lanes],
                own_node[y : y + 1, :HEAD],
                own_node[y : y + 1, HEAD:],
                peer_node[y : y + 1, :HEAD],
                peer_node[y : y + 1, HEAD:],
            )
            tail = jnp.zeros((TAIL, HEAD), F32)
            for t, term in enumerate(terms):
                tail = jnp.where(tail_row == t, term, tail)
            block = jnp.concatenate([mixed[half * 64 : half * 64 + 64, lanes], tail], axis=0)
            out[r * 8 + y] = block.astype(BF16)


def combine_kernel(path, got, out):
    core = lax.axis_index("core")
    x = lax.axis_index("x")
    y = lax.axis_index("y")
    logs = []
    for s in range(CHIPS):
        tail = got[s].astype(F32)[64:BLOCK]
        logs.append(tail[0:1] + tail[1:2] + tail[2:3])
    peak = logs[0]
    for s in range(1, CHIPS):
        peak = jnp.maximum(peak, logs[s])
    total = jnp.zeros((1, HEAD), F32)
    mixed = jnp.zeros((64, HEAD), F32)
    for s in range(CHIPS):
        share = jnp.exp2(logs[s] - peak)
        total = total + share
        mixed = mixed + share * got[s].astype(F32)[:64]
    mixed = mixed * (1.0 / total)
    tail_row = iota((TAIL, HEAD), 0)
    tail = jnp.zeros((TAIL, HEAD), F32)
    for j in range(2):
        node = path[y, 2 * x + j]
        held = got[node // 2].astype(F32)[64:BLOCK]
        is_own = node % 2 == core
        key = jnp.where(is_own, held[3:4], held[5:6])
        value = jnp.where(is_own, held[4:5], held[6:7])
        tail = jnp.where(tail_row == 2 * j, key, tail)
        tail = jnp.where(tail_row == 2 * j + 1, value, tail)
    block = jnp.concatenate([mixed, tail], axis=0).astype(BF16)
    for s in range(CHIPS):
        out[s] = block


def project_kernel(got, weight, peer, out):
    core = lax.axis_index("core")
    sides = []
    for h in range(2):
        own_h = [weight[(2 * p + h) * HEAD : (2 * p + h + 1) * HEAD, :] for p in range(4)]
        peer_h = []
        for p in range(4):
            at = (2 * p + h) * HEAD
            side = at // W_ROWS * HEAD
            peer_h.append(peer[at % W_ROWS : at % W_ROWS + HEAD, side : side + HEAD])
        sides.append(jnp.concatenate([jnp.concatenate(own_h, axis=0), jnp.concatenate(peer_h, axis=0)], axis=1))
    for r in range(HALF):
        a = got[pl.ds(r * 8, 8)][:, :64, :].reshape(LANES, HEAD)
        sums = dot(a, sides[0], 0, 0)[:NODES] + dot(a, sides[1], 0, 0)[NODES:]
        for t in range(8):
            rows = sums[t * 8 : t * 8 + 8]
            out[core * 8 + t, r] = rows[:, :HEAD]
            out[(1 - core) * 8 + t, r] = rows[:, HEAD:]


def sum_kernel(got, out):
    for core in range(2):
        total = got[core * 8]
        for t in range(1, 8):
            total = total + got[core * 8 + t]
        out[HALF * core : HALF * core + HALF] = total


def write_kernel(table, lengths, counts, spare, table_v, got, pool_in, pool, new_table, pages, sems):
    ctx = ctx_index()
    for r in range(REQUESTS):
        for p in range(PAGES_LOCAL):
            new_table[r, p] = table[r, p]
    row = iota((PAGE, 2 * HEAD), 0)
    for r in range(REQUESTS):
        length = lengths[r]
        count = counts[r]
        tail_page = length // PAGE
        for step in range(2):
            page = tail_page + step
            local = page - ctx * PAGES_LOCAL
            first = length - page * PAGE
            here = (local >= 0) & (local < PAGES_LOCAL)
            if step == 1:
                here = here & (first + count > 0)

            @pl.when(here)
            def _():
                slot = table[r, local]
                target = slot
                if step == 0:
                    uses = jnp.sum((table_v[...] == slot).astype(jnp.int32))
                    target = jnp.where(uses > 1, spare[r, 0], slot)
                    new_table[r, local] = target
                fetch = pltpu.make_async_copy(pool_in.at[slot], pages.at[2 * r + step], sems.at[2 * r + step])
                fetch.start()
                fetch.wait()
                now = pages[2 * r + step].astype(F32)
                for j in range(PATH_ROWS):
                    held = got[(j // 2) * 8 + r].astype(F32)[64:BLOCK]
                    at = 2 * (j % 2)
                    new = jnp.concatenate([held[at : at + 1], held[at + 1 : at + 2]], axis=1)
                    now = jnp.where((row == first + j) & (j < count), new, now)
                pages[2 * r + step] = now.astype(BF16)
                store = pltpu.make_async_copy(pages.at[2 * r + step], pool.at[target], sems.at[2 * r + step])
                store.start()
                store.wait()


def spec(space):
    return pl.BlockSpec(memory_space=space)


def on_device(queries, node_kv, pool, out_weight, parents, path, counts, lengths, table, free_slot):
    params = pltpu.CompilerParams(vmem_limit_bytes=LIMIT)
    shape = jax.ShapeDtypeStruct
    node = node_kv.reshape(REQUESTS, 2 * HEAD)
    held_pool, held_table, held_node, held_parents, held_weight, held_queries = (
        pltpu.with_memory_space_constraint(a, HBM)
        for a in (pool, table, node, parents, out_weight, queries.reshape(REQUESTS, 8 * HEAD))
    )

    message = pl.pallas_call(
        message_kernel,
        out_shape=shape((2 * CHIPS, HALF * 8, HEAD), BF16),
        in_specs=[spec(VMEM)],
        out_specs=spec(VMEM),
        compiler_params=params,
        name="message",
    )(held_queries)
    every_query = lax.all_to_all(message, ("x", "y", "core"), 0, 0, tiled=True)

    *sends, own, pool_copy, mask = pl.pallas_call(
        prepare_kernel,
        out_shape=(
            *(shape((NODE_ROWS0 + extra, 2 * HEAD), BF16) for extra in (16, W_ROWS)),
            shape((HALF * SPAN, 2 * HEAD), BF16),
            shape(pool.shape, pool.dtype),
            shape((HALF, 16, 2 * NODES), F32),
        ),
        in_specs=[spec(SMEM), spec(HBM), spec(VMEM), spec(VMEM), spec(HBM)],
        out_specs=(*([spec(VMEM)] * (SENDS + 1)), spec(HBM), spec(VMEM)),
        scratch_shapes=[VMEM(pool.shape, BF16), pltpu.SemaphoreType.DMA((68,))],
        compiler_params=params,
        cost_estimate=pl.CostEstimate(flops=50_000_000, bytes_accessed=7_000_000, transcendentals=0),
        name="prepare",
    )(held_table, held_pool, held_node, held_parents, held_weight)
    peers = [lax.ppermute(a, "core", [(0, 1), (1, 0)]) for a in sends]
    mask, *peers = lax.optimization_barrier((mask, *peers))

    partial = pl.pallas_call(
        attend_kernel,
        out_shape=shape((CHIPS, BLOCK, HEAD), BF16),
        in_specs=[spec(SMEM)] + [spec(VMEM)] * (4 + SENDS),
        out_specs=spec(VMEM),
        compiler_params=params,
        name="attend",
    )(lengths, every_query, own, node, mask, *peers)

    parts = lax.all_to_all(partial, ("x", "y"), 0, 0, tiled=True)
    mixed = pl.pallas_call(
        combine_kernel,
        out_shape=shape((CHIPS, BLOCK, HEAD), BF16),
        in_specs=[spec(SMEM), spec(VMEM)],
        out_specs=spec(VMEM),
        compiler_params=params,
        name="combine",
    )(path, parts)
    attention = lax.all_to_all(mixed, ("x", "y"), 0, 0, tiled=True)

    sums = pl.pallas_call(
        project_kernel,
        grid=(1,),
        out_shape=shape((16, HALF, 8, HEAD), F32),
        in_specs=[
            pl.BlockSpec((CHIPS, BLOCK, HEAD), lambda i: (0, 0, 0)),
            pl.BlockSpec((8 * HEAD, HEAD), lambda i: (0, 0)),
            pl.BlockSpec((W_ROWS, 2 * HEAD), lambda i: (0, 0)),
        ],
        out_specs=pl.BlockSpec((16, HALF, 8, HEAD), lambda i: (0, 0, 0, 0)),
        compiler_params=params,
        name="project",
    )(attention, out_weight, peers[1])
    shares = lax.all_to_all(sums, ("core", "tp"), 0, 0, tiled=True)
    projected = pl.pallas_call(
        sum_kernel,
        out_shape=shape((REQUESTS, 8, HEAD), F32),
        in_specs=[spec(VMEM)],
        out_specs=spec(VMEM),
        compiler_params=params,
        name="sum",
    )(shares)

    updated_pool, new_table = pl.pallas_call(
        write_kernel,
        out_shape=(shape(pool.shape, pool.dtype), shape(table.shape, table.dtype)),
        in_specs=[spec(SMEM)] * 4 + [spec(VMEM), spec(VMEM), spec(HBM)],
        out_specs=(spec(HBM), spec(SMEM)),
        input_output_aliases={6: 0},
        scratch_shapes=[VMEM((2 * REQUESTS, PAGE, 2 * HEAD), BF16), pltpu.SemaphoreType.DMA((2 * REQUESTS,))],
        compiler_params=params,
        name="write",
    )(table, lengths, counts, free_slot, table, attention, pool_copy)
    return projected, updated_pool, new_table


def solution(mesh):
    fine = Mesh(mesh.devices.reshape(4, 8, 2, 8), ("x", "y", "core", "tp"))
    ctx = ("x", "y", "core")
    placed = (
        P(None, ctx, "tp"),
        P(None, ctx, "tp"),
        P(ctx, None, "tp"),
        P("tp", ctx),
        P(),
        P(),
        P(),
        P(),
        P(None, ctx),
        P(None, ctx),
    )
    return jax.shard_map(
        on_device,
        mesh=fine,
        in_specs=placed,
        out_specs=(P(None, "tp", ctx), P(ctx, None, "tp"), P(None, ctx)),
        check_vma=False,
    )
```

```python
import jax
import jax.numpy as jnp
from jax import lax
from jax.experimental import pallas as pl
from jax.experimental.pallas import tpu as pltpu
from jax.sharding import Mesh, PartitionSpec as P

F32 = jnp.float32
BF16 = jnp.bfloat16

HEAD = 128
PATH_ROWS = 8
PAGE = 64
REQUESTS = 8
HALF = 4
NODES = 64
PAGES_LOCAL = 8
SPAN = PAGE * PAGES_LOCAL
LANES = 8 * NODES
CHIPS = 32
TAIL = 8
BLOCK = 64 + TAIL
DEAD = -1e30
FLOOR = -1e28
LOG2E = 1.4426950408889634
SCALE2 = HEAD ** (-0.5) * LOG2E

SENDS = 2
EACH = HALF // SENDS
NODE_ROWS0 = EACH * SPAN
W_ROWS = 512

VMEM = pltpu.VMEM
SMEM = pltpu.SMEM
HBM = pltpu.HBM
LIMIT = 40 * 1024 * 1024


def iota(shape, dim):
    return lax.broadcasted_iota(jnp.int32, shape, dim)


def dot(a, b, ca=1, cb=0):
    return lax.dot_general(a, b, (((ca,), (cb,)), ((), ())), preferred_element_type=F32)


def ctx_index():
    return (lax.axis_index("x") * 8 + lax.axis_index("y")) * 2 + lax.axis_index("core")


def position():
    return lax.axis_index("core"), ctx_index()


def message_kernel(query, message):
    flat = query[...].astype(F32)
    for half in range(2):
        rows = [
            flat[r : r + 1, h * HEAD : (h + 1) * HEAD] for r in range(HALF * half, HALF * half + HALF) for h in range(8)
        ]
        rows = jnp.concatenate(rows, axis=0).astype(BF16)
        for chip in range(CHIPS):
            message[CHIPS * half + chip] = rows


def prepare_kernel(table, pool, node, parents, weight, send0, send1, own, pool_copy, mask, held, sems):
    core, ctx = position()
    copies = []
    sends = (send0, send1)
    for mine in range(2):
        for r in range(HALF):
            for p in range(PAGES_LOCAL):
                slot = table[HALF * (core if mine else 1 - core) + r, p]
                to, n = (own, r * PAGES_LOCAL + p) if mine else (sends[r // EACH], (r % EACH) * PAGES_LOCAL + p)
                if not mine and r >= EACH:
                    n += PAGES_LOCAL
                at = mine * 32 + r * PAGES_LOCAL + p
                copies.append(pltpu.make_async_copy(pool.at[slot], to.at[pl.ds(n * PAGE, PAGE), :], sems.at[at]))
    for half in range(2):
        copies.append(
            pltpu.make_async_copy(
                weight.at[pl.ds(half * W_ROWS, W_ROWS), :],
                send1.at[pl.ds(0, W_ROWS), pl.ds(half * HEAD, HEAD)],
                sems.at[66 + half],
            )
        )
    fetch = pltpu.make_async_copy(pool, held, sems.at[64])
    for c in copies:
        c.start()
    fetch.start()
    rows = node[...].astype(F32)
    send0[pl.ds(NODE_ROWS0, 16), :] = jnp.concatenate([rows, jnp.zeros_like(rows)], axis=0).astype(BF16)
    up = iota((NODES, NODES), 0)
    down = iota((NODES, NODES), 1)
    twice = (iota((NODES, 2 * NODES), 0) == iota((NODES, 2 * NODES), 1) % NODES).astype(F32).astype(BF16)
    pick_row = iota((16, NODES), 0)
    pick_node = iota((16, NODES), 1)
    reach = []
    for r in range(HALF):
        link = parents[pl.ds(HALF * core + r, 1), :]
        reach.append(((up == link) | (up == down)).astype(F32).astype(BF16))
    for step in range(6):
        reach = [jnp.minimum(dot(m, m), 1.0).astype(BF16) for m in reach]
        if step == 2:
            fetch.wait()
            store = pltpu.make_async_copy(held, pool_copy, sems.at[65])
            store.start()
    for r in range(HALF):
        mine = HALF * core + r
        pick = ((pick_row == mine) & (pick_node == ctx)) | (
            (pick_row == REQUESTS + mine) & (pick_node == ctx + 1 - 2 * core)
        )
        seen = dot(pick.astype(F32).astype(BF16), reach[r]).astype(BF16)
        mask[r] = dot(seen, twice)
    for c in copies:
        c.wait()
    store.wait()


def attend_kernel(lengths, queries, own, node, mask, peer0, peer1, out):
    core, ctx = position()
    lane = iota((LANES, LANES), 1)
    asker = lane % NODES
    came = (asker % 2) * CHIPS + (asker // 2 % 8) * 4 + asker // 16
    order = (iota((LANES, LANES), 0) == came * 8 + lane // NODES).astype(F32).astype(BF16)
    peers = (peer0, peer1)
    peer_node = peer0[pl.ds(NODE_ROWS0, 16), :].astype(F32)[:REQUESTS]
    own_node = node[...].astype(F32)
    nodes = jnp.concatenate([own_node, peer_node], axis=0).astype(BF16)
    ones = jnp.ones((16, SPAN), BF16)
    ones_tree = jnp.ones((16, 16), BF16)
    row = iota((SPAN, LANES), 0)
    tail_row = iota((TAIL, HEAD), 0)
    def scores(r):
        part = queries[:, pl.ds((r // 2) * 16, 16), :].astype(F32)[:, (r % 2) * 8 : (r % 2) * 8 + 8, :]
        part = part.reshape(LANES, HEAD).astype(BF16)
        query = dot(part, order, 0, 0).astype(BF16)
        length = lengths[HALF * core + r]
        span_own = own[pl.ds(r * SPAN, SPAN), :]
        span_peer = peers[r // EACH][pl.ds((r // EACH + r % EACH) * SPAN, SPAN), :]
        live_own = row < length - ctx * SPAN
        live_peer = row < length - (ctx + 1 - 2 * core) * SPAN
        seen = jnp.concatenate([mask[r]] * 4, axis=1)
        s_own = jnp.where(live_own, dot(span_own[:, :HEAD], query), DEAD)
        s_peer = jnp.where(live_peer, dot(span_peer[:, :HEAD], query), DEAD)
        s_tree = jnp.where(seen > 0.5, dot(nodes[:, :HEAD], query), DEAD)
        peak = jnp.maximum(
            jnp.maximum(jnp.max(s_own, axis=0, keepdims=True), jnp.max(s_peer, axis=0, keepdims=True)),
            jnp.max(s_tree, axis=0, keepdims=True),
        )
        peak = jnp.maximum(peak, FLOOR) * SCALE2
        return s_own, s_peer, s_tree, span_own, span_peer, peak

    ahead = scores(0)
    for r in range(HALF):
        s_own, s_peer, s_tree, span_own, span_peer, peak = ahead
        if r + 1 < HALF:
            ahead = scores(r + 1)
        total = None
        for s, v, one in (
            (s_own, span_own[:, HEAD:], ones),
            (s_peer, span_peer[:, HEAD:], ones),
            (s_tree, nodes[:, HEAD:], ones_tree),
        ):
            p = jnp.exp2(s * SCALE2 - peak)
            lhs = jnp.concatenate([v.astype(F32).T.astype(BF16), one], axis=0)
            high = p.astype(BF16)
            low = (p - high.astype(F32)).astype(BF16)
            add = dot(lhs, high) + dot(lhs, low)
            total = add if total is None else total + add
        row_sum = total[HEAD : HEAD + 1]
        some = row_sum > 0.0
        mixed = total[:HEAD] * (1.0 / jnp.where(some, row_sum, 1.0))
        log_sum = jnp.where(some, peak + jnp.log2(jnp.where(some, row_sum, 1.0)), DEAD)
        first = log_sum.astype(BF16).astype(F32)
        rest = log_sum - first
        second = rest.astype(BF16).astype(F32)
        third = rest - second
        for y in range(8):
            lanes = slice((y // 2) * HEAD, (y // 2 + 1) * HEAD)
            half = y % 2
            terms = (
                first[:, lanes],
                second[:, lanes],
                third[:, lanes],
                own_node[y : y + 1, :HEAD],
                own_node[y : y + 1, HEAD:],
                peer_node[y : y + 1, :HEAD],
                peer_node[y : y + 1, HEAD:],
            )
            tail = jnp.zeros((TAIL, HEAD), F32)
            for t, term in enumerate(terms):
                tail = jnp.where(tail_row == t, term, tail)
            block = jnp.concatenate([mixed[half * 64 : half * 64 + 64, lanes], tail], axis=0)
            out[r * 8 + y] = block.astype(BF16)


def combine_kernel(path, got, out):
    core = lax.axis_index("core")
    x = lax.axis_index("x")
    y = lax.axis_index("y")
    logs = []
    for s in range(CHIPS):
        tail = got[s].astype(F32)[64:BLOCK]
        logs.append(tail[0:1] + tail[1:2] + tail[2:3])
    peak = logs[0]
    for s in range(1, CHIPS):
        peak = jnp.maximum(peak, logs[s])
    total = jnp.zeros((1, HEAD), F32)
    mixed = jnp.zeros((64, HEAD), F32)
    for s in range(CHIPS):
        share = jnp.exp2(logs[s] - peak)
        total = total + share
        mixed = mixed + share * got[s].astype(F32)[:64]
    mixed = mixed * (1.0 / total)
    tail_row = iota((TAIL, HEAD), 0)
    tail = jnp.zeros((TAIL, HEAD), F32)
    for j in range(2):
        node = path[y, 2 * x + j]
        held = got[node // 2].astype(F32)[64:BLOCK]
        is_own = node % 2 == core
        key = jnp.where(is_own, held[3:4], held[5:6])
        value = jnp.where(is_own, held[4:5], held[6:7])
        tail = jnp.where(tail_row == 2 * j, key, tail)
        tail = jnp.where(tail_row == 2 * j + 1, value, tail)
    block = jnp.concatenate([mixed, tail], axis=0).astype(BF16)
    for s in range(CHIPS):
        out[s] = block


def project_kernel(got, weight, peer, out):
    core = lax.axis_index("core")
    sides = []
    for h in range(2):
        own_h = [weight[(2 * p + h) * HEAD : (2 * p + h + 1) * HEAD, :] for p in range(4)]
        peer_h = []
        for p in range(4):
            at = (2 * p + h) * HEAD
            side = at // W_ROWS * HEAD
            peer_h.append(peer[at % W_ROWS : at % W_ROWS + HEAD, side : side + HEAD])
        sides.append(jnp.concatenate([jnp.concatenate(own_h, axis=0), jnp.concatenate(peer_h, axis=0)], axis=1))
    for r in range(HALF):
        a = got[pl.ds(r * 8, 8)][:, :64, :].reshape(LANES, HEAD)
        sums = dot(a, sides[0], 0, 0)[:NODES] + dot(a, sides[1], 0, 0)[NODES:]
        for t in range(8):
            rows = sums[t * 8 : t * 8 + 8]
            out[core * 8 + t, r] = rows[:, :HEAD]
            out[(1 - core) * 8 + t, r] = rows[:, HEAD:]


def sum_kernel(got, out):
    for core in range(2):
        total = got[core * 8]
        for t in range(1, 8):
            total = total + got[core * 8 + t]
        out[HALF * core : HALF * core + HALF] = total


def write_kernel(table, lengths, counts, spare, table_v, got, pool_in, pool, new_table, pages, sems):
    ctx = ctx_index()
    for r in range(REQUESTS):
        for p in range(PAGES_LOCAL):
            new_table[r, p] = table[r, p]
    row = iota((PAGE, 2 * HEAD), 0)
    for r in range(REQUESTS):
        length = lengths[r]
        count = counts[r]
        tail_page = length // PAGE
        for step in range(2):
            page = tail_page + step
            local = page - ctx * PAGES_LOCAL
            first = length - page * PAGE
            here = (local >= 0) & (local < PAGES_LOCAL)
            if step == 1:
                here = here & (first + count > 0)

            @pl.when(here)
            def _():
                slot = table[r, local]
                target = slot
                if step == 0:
                    uses = jnp.sum((table_v[...] == slot).astype(jnp.int32))
                    target = jnp.where(uses > 1, spare[r, 0], slot)
                    new_table[r, local] = target
                fetch = pltpu.make_async_copy(pool_in.at[slot], pages.at[2 * r + step], sems.at[2 * r + step])
                fetch.start()
                fetch.wait()
                now = pages[2 * r + step].astype(F32)
                for j in range(PATH_ROWS):
                    held = got[(j // 2) * 8 + r].astype(F32)[64:BLOCK]
                    at = 2 * (j % 2)
                    new = jnp.concatenate([held[at : at + 1], held[at + 1 : at + 2]], axis=1)
                    now = jnp.where((row == first + j) & (j < count), new, now)
                pages[2 * r + step] = now.astype(BF16)
                store = pltpu.make_async_copy(pages.at[2 * r + step], pool.at[target], sems.at[2 * r + step])
                store.start()
                store.wait()


def spec(space):
    return pl.BlockSpec(memory_space=space)


def on_device(queries, node_kv, pool, out_weight, parents, path, counts, lengths, table, free_slot):
    params = pltpu.CompilerParams(vmem_limit_bytes=LIMIT)
    shape = jax.ShapeDtypeStruct
    node = node_kv.reshape(REQUESTS, 2 * HEAD)
    held_pool, held_table, held_node, held_parents, held_weight, held_queries = (
        pltpu.with_memory_space_constraint(a, HBM)
        for a in (pool, table, node, parents, out_weight, queries.reshape(REQUESTS, 8 * HEAD))
    )

    message = pl.pallas_call(
        message_kernel,
        out_shape=shape((2 * CHIPS, HALF * 8, HEAD), BF16),
        in_specs=[spec(VMEM)],
        out_specs=spec(VMEM),
        compiler_params=params,
        name="message",
    )(held_queries)
    every_query = lax.all_to_all(message, ("core", "y", "x"), 0, 0, tiled=True)

    *sends, own, pool_copy, mask = pl.pallas_call(
        prepare_kernel,
        out_shape=(
            *(shape((NODE_ROWS0 + extra, 2 * HEAD), BF16) for extra in (16, W_ROWS)),
            shape((HALF * SPAN, 2 * HEAD), BF16),
            shape(pool.shape, pool.dtype),
            shape((HALF, 16, 2 * NODES), F32),
        ),
        in_specs=[spec(SMEM), spec(HBM), spec(VMEM), spec(VMEM), spec(HBM)],
        out_specs=(*([spec(VMEM)] * (SENDS + 1)), spec(HBM), spec(VMEM)),
        scratch_shapes=[VMEM(pool.shape, BF16), pltpu.SemaphoreType.DMA((68,))],
        compiler_params=params,
        cost_estimate=pl.CostEstimate(flops=50_000_000, bytes_accessed=7_000_000, transcendentals=0),
        name="prepare",
    )(held_table, held_pool, held_node, held_parents, held_weight)
    peers = [lax.ppermute(a, "core", [(0, 1), (1, 0)]) for a in sends]
    mask, *peers = lax.optimization_barrier((mask, *peers))

    partial = pl.pallas_call(
        attend_kernel,
        out_shape=shape((CHIPS, BLOCK, HEAD), BF16),
        in_specs=[spec(SMEM)] + [spec(VMEM)] * (4 + SENDS),
        out_specs=spec(VMEM),
        compiler_params=params,
        name="attend",
    )(lengths, every_query, own, node, mask, *peers)

    parts = lax.all_to_all(partial, ("x", "y"), 0, 0, tiled=True)
    mixed = pl.pallas_call(
        combine_kernel,
        out_shape=shape((CHIPS, BLOCK, HEAD), BF16),
        in_specs=[spec(SMEM), spec(VMEM)],
        out_specs=spec(VMEM),
        compiler_params=params,
        name="combine",
    )(path, parts)
    attention = lax.all_to_all(mixed, ("x", "y"), 0, 0, tiled=True)

    sums = pl.pallas_call(
        project_kernel,
        grid=(1,),
        out_shape=shape((16, HALF, 8, HEAD), F32),
        in_specs=[
            pl.BlockSpec((CHIPS, BLOCK, HEAD), lambda i: (0, 0, 0)),
            pl.BlockSpec((8 * HEAD, HEAD), lambda i: (0, 0)),
            pl.BlockSpec((W_ROWS, 2 * HEAD), lambda i: (0, 0)),
        ],
        out_specs=pl.BlockSpec((16, HALF, 8, HEAD), lambda i: (0, 0, 0, 0)),
        compiler_params=params,
        name="project",
    )(attention, out_weight, peers[1])
    shares = lax.all_to_all(sums, ("core", "tp"), 0, 0, tiled=True)
    projected = pl.pallas_call(
        sum_kernel,
        out_shape=shape((REQUESTS, 8, HEAD), F32),
        in_specs=[spec(VMEM)],
        out_specs=spec(VMEM),
        compiler_params=params,
        name="sum",
    )(shares)

    updated_pool, new_table = pl.pallas_call(
        write_kernel,
        out_shape=(shape(pool.shape, pool.dtype), shape(table.shape, table.dtype)),
        in_specs=[spec(SMEM)] * 4 + [spec(VMEM), spec(VMEM), spec(HBM)],
        out_specs=(spec(HBM), spec(SMEM)),
        input_output_aliases={6: 0},
        scratch_shapes=[VMEM((2 * REQUESTS, PAGE, 2 * HEAD), BF16), pltpu.SemaphoreType.DMA((2 * REQUESTS,))],
        compiler_params=params,
        name="write",
    )(table, lengths, counts, free_slot, table, attention, pool_copy)
    return projected, updated_pool, new_table


def solution(mesh):
    fine = Mesh(mesh.devices.reshape(4, 8, 2, 8), ("x", "y", "core", "tp"))
    ctx = ("x", "y", "core")
    placed = (
        P(None, ctx, "tp"),
        P(None, ctx, "tp"),
        P(ctx, None, "tp"),
        P("tp", ctx),
        P(),
        P(),
        P(),
        P(),
        P(None, ctx),
        P(None, ctx),
    )
    return jax.shard_map(
        on_device,
        mesh=fine,
        in_specs=placed,
        out_specs=(P(None, "tp", ctx), P(ctx, None, "tp"), P(None, ctx)),
        check_vma=False,
    )
```

```python
import jax
import jax.numpy as jnp
from jax import lax
from jax.experimental import pallas as pl
from jax.experimental.pallas import tpu as pltpu
from jax.sharding import Mesh, PartitionSpec as P

F32 = jnp.float32
BF16 = jnp.bfloat16

HEAD = 128
PATH_ROWS = 8
PAGE = 64
REQUESTS = 8
HALF = 4
NODES = 64
PAGES_LOCAL = 8
SPAN = PAGE * PAGES_LOCAL
LANES = 8 * NODES
CHIPS = 32
TAIL = 8
BLOCK = 64 + TAIL
DEAD = -1e30
FLOOR = -1e28
LOG2E = 1.4426950408889634
SCALE2 = HEAD ** (-0.5) * LOG2E

SENDS = 2
EACH = HALF // SENDS
NODE_ROWS0 = EACH * SPAN
W_ROWS = 512

VMEM = pltpu.VMEM
SMEM = pltpu.SMEM
HBM = pltpu.HBM
LIMIT = 40 * 1024 * 1024


def iota(shape, dim):
    return lax.broadcasted_iota(jnp.int32, shape, dim)


def dot(a, b, ca=1, cb=0):
    return lax.dot_general(a, b, (((ca,), (cb,)), ((), ())), preferred_element_type=F32)


def ctx_index():
    return (lax.axis_index("x") * 8 + lax.axis_index("y")) * 2 + lax.axis_index("core")


def position():
    return lax.axis_index("core"), ctx_index()


def message_kernel(query, message):
    flat = query[...].astype(F32)
    for half in range(2):
        rows = [
            flat[r : r + 1, h * HEAD : (h + 1) * HEAD] for r in range(HALF * half, HALF * half + HALF) for h in range(8)
        ]
        rows = jnp.concatenate(rows, axis=0).astype(BF16)
        for chip in range(CHIPS):
            message[2 * chip + half] = rows


def prepare_kernel(table, pool, node, parents, weight, send0, send1, own, pool_copy, mask, order, turned, held, sems):
    core, ctx = position()
    copies = []
    sends = (send0, send1)
    for mine in range(2):
        for r in range(HALF):
            for p in range(PAGES_LOCAL):
                slot = table[HALF * (core if mine else 1 - core) + r, p]
                to, n = (own, r * PAGES_LOCAL + p) if mine else (sends[r // EACH], (r % EACH) * PAGES_LOCAL + p)
                if not mine and r >= EACH:
                    n += PAGES_LOCAL
                at = mine * 32 + r * PAGES_LOCAL + p
                copies.append(pltpu.make_async_copy(pool.at[slot], to.at[pl.ds(n * PAGE, PAGE), :], sems.at[at]))
    for half in range(2):
        copies.append(
            pltpu.make_async_copy(
                weight.at[pl.ds(half * W_ROWS, W_ROWS), :],
                send1.at[pl.ds(0, W_ROWS), pl.ds(half * HEAD, HEAD)],
                sems.at[66 + half],
            )
        )
    fetch = pltpu.make_async_copy(pool, held, sems.at[64])
    for c in copies:
        c.start()
    fetch.start()
    rows = node[...].astype(F32)
    send0[pl.ds(NODE_ROWS0, 16), :] = jnp.concatenate([rows, jnp.zeros_like(rows)], axis=0).astype(BF16)
    up = iota((NODES, NODES), 0)
    down = iota((NODES, NODES), 1)
    twice = (iota((NODES, 2 * NODES), 0) == iota((NODES, 2 * NODES), 1) % NODES).astype(F32).astype(BF16)
    pick_row = iota((16, NODES), 0)
    pick_node = iota((16, NODES), 1)
    reach = []
    for r in range(HALF):
        link = parents[pl.ds(HALF * core + r, 1), :]
        reach.append(((up == link) | (up == down)).astype(F32).astype(BF16))
    for step in range(6):
        reach = [jnp.minimum(dot(m, m), 1.0).astype(BF16) for m in reach]
        if step == 2:
            fetch.wait()
            store = pltpu.make_async_copy(held, pool_copy, sems.at[65])
            store.start()
    for r in range(HALF):
        mine = HALF * core + r
        pick = ((pick_row == mine) & (pick_node == ctx)) | (
            (pick_row == REQUESTS + mine) & (pick_node == ctx + 1 - 2 * core)
        )
        seen = dot(pick.astype(F32).astype(BF16), reach[r]).astype(BF16)
        mask[r] = dot(seen, twice)
    lane = iota((LANES, LANES), 1)
    order[...] = (iota((LANES, LANES), 0) == (lane % NODES) * 8 + lane // NODES).astype(F32).astype(BF16)
    for c in copies:
        c.wait()
    ones = jnp.ones((16, SPAN), BF16)
    for r in range(HALF):
        values = own[pl.ds(r * SPAN, SPAN), :][:, HEAD:].astype(F32).T.astype(BF16)
        turned[r] = jnp.concatenate([values, ones], axis=0)
    store.wait()


def attend_kernel(lengths, queries, own, node, mask, order_in, turned, peer0, peer1, out):
    core, ctx = position()
    order = order_in[...]
    peers = (peer0, peer1)
    peer_node = peer0[pl.ds(NODE_ROWS0, 16), :].astype(F32)[:REQUESTS]
    own_node = node[...].astype(F32)
    nodes = jnp.concatenate([own_node, peer_node], axis=0).astype(BF16)
    ones = jnp.ones((16, SPAN), BF16)
    ones_tree = jnp.ones((16, 16), BF16)
    row = iota((SPAN, LANES), 0)
    tail_row = iota((TAIL, HEAD), 0)
    def scores(r):
        part = queries[:, pl.ds((r // 2) * 16, 16), :].astype(F32)[:, (r % 2) * 8 : (r % 2) * 8 + 8, :]
        part = part.reshape(LANES, HEAD).astype(BF16)
        query = dot(part, order, 0, 0).astype(BF16)
        length = lengths[HALF * core + r]
        span_own = own[pl.ds(r * SPAN, SPAN), :]
        span_peer = peers[r // EACH][pl.ds((r // EACH + r % EACH) * SPAN, SPAN), :]
        live_own = row < length - ctx * SPAN
        live_peer = row < length - (ctx + 1 - 2 * core) * SPAN
        seen = jnp.concatenate([mask[r]] * 4, axis=1)
        s_own = jnp.where(live_own, dot(span_own[:, :HEAD], query), DEAD)
        s_peer = jnp.where(live_peer, dot(span_peer[:, :HEAD], query), DEAD)
        s_tree = jnp.where(seen > 0.5, dot(nodes[:, :HEAD], query), DEAD)
        peak = jnp.maximum(
            jnp.maximum(jnp.max(s_own, axis=0, keepdims=True), jnp.max(s_peer, axis=0, keepdims=True)),
            jnp.max(s_tree, axis=0, keepdims=True),
        )
        peak = jnp.maximum(peak, FLOOR) * SCALE2
        return s_own, s_peer, s_tree, span_own, span_peer, peak

    ahead = scores(0)
    for r in range(HALF):
        s_own, s_peer, s_tree, span_own, span_peer, peak = ahead
        if r + 1 < HALF:
            ahead = scores(r + 1)
        total = None
        for s, v, one in (
            (s_own, None, turned[r]),
            (s_peer, span_peer[:, HEAD:], ones),
            (s_tree, nodes[:, HEAD:], ones_tree),
        ):
            p = jnp.exp2(s * SCALE2 - peak)
            lhs = one if v is None else jnp.concatenate([v.astype(F32).T.astype(BF16), one], axis=0)
            high = p.astype(BF16)
            low = (p - high.astype(F32)).astype(BF16)
            add = dot(lhs, high) + dot(lhs, low)
            total = add if total is None else total + add
        row_sum = total[HEAD : HEAD + 1]
        some = row_sum > 0.0
        mixed = total[:HEAD] * (1.0 / jnp.where(some, row_sum, 1.0))
        log_sum = jnp.where(some, peak + jnp.log2(jnp.where(some, row_sum, 1.0)), DEAD)
        first = log_sum.astype(BF16).astype(F32)
        rest = log_sum - first
        second = rest.astype(BF16).astype(F32)
        third = rest - second
        for y in range(8):
            lanes = slice((y // 2) * HEAD, (y // 2 + 1) * HEAD)
            half = y % 2
            terms = (
                first[:, lanes],
                second[:, lanes],
                third[:, lanes],
                own_node[y : y + 1, :HEAD],
                own_node[y : y + 1, HEAD:],
                peer_node[y : y + 1, :HEAD],
                peer_node[y : y + 1, HEAD:],
            )
            tail = jnp.zeros((TAIL, HEAD), F32)
            for t, term in enumerate(terms):
                tail = jnp.where(tail_row == t, term, tail)
            block = jnp.concatenate([mixed[half * 64 : half * 64 + 64, lanes], tail], axis=0)
            out[r * 8 + y] = block.astype(BF16)


def combine_kernel(path, got, out):
    core = lax.axis_index("core")
    x = lax.axis_index("x")
    y = lax.axis_index("y")
    logs = []
    for s in range(CHIPS):
        tail = got[s].astype(F32)[64:BLOCK]
        logs.append(tail[0:1] + tail[1:2] + tail[2:3])
    peak = logs[0]
    for s in range(1, CHIPS):
        peak = jnp.maximum(peak, logs[s])
    total = jnp.zeros((1, HEAD), F32)
    mixed = jnp.zeros((64, HEAD), F32)
    for s in range(CHIPS):
        share = jnp.exp2(logs[s] - peak)
        total = total + share
        mixed = mixed + share * got[s].astype(F32)[:64]
    mixed = mixed * (1.0 / total)
    tail_row = iota((TAIL, HEAD), 0)
    tail = jnp.zeros((TAIL, HEAD), F32)
    for j in range(2):
        node = path[y, 2 * x + j]
        held = got[node // 2].astype(F32)[64:BLOCK]
        is_own = node % 2 == core
        key = jnp.where(is_own, held[3:4], held[5:6])
        value = jnp.where(is_own, held[4:5], held[6:7])
        tail = jnp.where(tail_row == 2 * j, key, tail)
        tail = jnp.where(tail_row == 2 * j + 1, value, tail)
    block = jnp.concatenate([mixed, tail], axis=0).astype(BF16)
    for s in range(CHIPS):
        out[s] = block


def project_kernel(got, weight, peer, out):
    core = lax.axis_index("core")
    sides = []
    for h in range(2):
        own_h = [weight[(2 * p + h) * HEAD : (2 * p + h + 1) * HEAD, :] for p in range(4)]
        peer_h = []
        for p in range(4):
            at = (2 * p + h) * HEAD
            side = at // W_ROWS * HEAD
            peer_h.append(peer[at % W_ROWS : at % W_ROWS + HEAD, side : side + HEAD])
        sides.append(jnp.concatenate([jnp.concatenate(own_h, axis=0), jnp.concatenate(peer_h, axis=0)], axis=1))
    for r in range(HALF):
        a = got[pl.ds(r * 8, 8)][:, :64, :].reshape(LANES, HEAD)
        sums = dot(a, sides[0], 0, 0)[:NODES] + dot(a, sides[1], 0, 0)[NODES:]
        for t in range(8):
            rows = sums[t * 8 : t * 8 + 8]
            out[core * 8 + t, r] = rows[:, :HEAD]
            out[(1 - core) * 8 + t, r] = rows[:, HEAD:]


def sum_kernel(got, out):
    for core in range(2):
        total = got[core * 8]
        for t in range(1, 8):
            total = total + got[core * 8 + t]
        out[HALF * core : HALF * core + HALF] = total


def write_kernel(table, lengths, counts, spare, table_v, got, pool_in, pool, new_table, pages, sems):
    ctx = ctx_index()
    for r in range(REQUESTS):
        for p in range(PAGES_LOCAL):
            new_table[r, p] = table[r, p]
    row = iota((PAGE, 2 * HEAD), 0)
    for r in range(REQUESTS):
        length = lengths[r]
        count = counts[r]
        tail_page = length // PAGE
        for step in range(2):
            page = tail_page + step
            local = page - ctx * PAGES_LOCAL
            first = length - page * PAGE
            here = (local >= 0) & (local < PAGES_LOCAL)
            if step == 1:
                here = here & (first + count > 0)

            @pl.when(here)
            def _():
                slot = table[r, local]
                target = slot
                if step == 0:
                    uses = jnp.sum((table_v[...] == slot).astype(jnp.int32))
                    target = jnp.where(uses > 1, spare[r, 0], slot)
                    new_table[r, local] = target
                fetch = pltpu.make_async_copy(pool_in.at[slot], pages.at[2 * r + step], sems.at[2 * r + step])
                fetch.start()
                fetch.wait()
                now = pages[2 * r + step].astype(F32)
                for j in range(PATH_ROWS):
                    held = got[(j // 2) * 8 + r].astype(F32)[64:BLOCK]
                    at = 2 * (j % 2)
                    new = jnp.concatenate([held[at : at + 1], held[at + 1 : at + 2]], axis=1)
                    now = jnp.where((row == first + j) & (j < count), new, now)
                pages[2 * r + step] = now.astype(BF16)
                store = pltpu.make_async_copy(pages.at[2 * r + step], pool.at[target], sems.at[2 * r + step])
                store.start()
                store.wait()


def spec(space):
    return pl.BlockSpec(memory_space=space)


def on_device(queries, node_kv, pool, out_weight, parents, path, counts, lengths, table, free_slot):
    params = pltpu.CompilerParams(vmem_limit_bytes=LIMIT)
    shape = jax.ShapeDtypeStruct
    node = node_kv.reshape(REQUESTS, 2 * HEAD)
    held_pool, held_table, held_node, held_parents, held_weight, held_queries = (
        pltpu.with_memory_space_constraint(a, HBM)
        for a in (pool, table, node, parents, out_weight, queries.reshape(REQUESTS, 8 * HEAD))
    )

    message = pl.pallas_call(
        message_kernel,
        out_shape=shape((2 * CHIPS, HALF * 8, HEAD), BF16),
        in_specs=[spec(VMEM)],
        out_specs=spec(VMEM),
        compiler_params=params,
        name="message",
    )(held_queries)
    every_query = lax.all_to_all(message, ("x", "y", "core"), 0, 0, tiled=True)

    *sends, own, pool_copy, mask, order, turned = pl.pallas_call(
        prepare_kernel,
        out_shape=(
            *(shape((NODE_ROWS0 + extra, 2 * HEAD), BF16) for extra in (16, W_ROWS)),
            shape((HALF * SPAN, 2 * HEAD), BF16),
            shape(pool.shape, pool.dtype),
            shape((HALF, 16, 2 * NODES), F32),
            shape((LANES, LANES), BF16),
            shape((HALF, HEAD + 16, SPAN), BF16),
        ),
        in_specs=[spec(SMEM), spec(HBM), spec(VMEM), spec(VMEM), spec(HBM)],
        out_specs=(*([spec(VMEM)] * (SENDS + 1)), spec(HBM), spec(VMEM), spec(VMEM), spec(VMEM)),
        scratch_shapes=[VMEM(pool.shape, BF16), pltpu.SemaphoreType.DMA((68,))],
        compiler_params=params,
        cost_estimate=pl.CostEstimate(flops=50_000_000, bytes_accessed=7_000_000, transcendentals=0),
        name="prepare",
    )(held_table, held_pool, held_node, held_parents, held_weight)
    peers = [lax.ppermute(a, "core", [(0, 1), (1, 0)]) for a in sends]
    mask, *peers = lax.optimization_barrier((mask, *peers))

    partial = pl.pallas_call(
        attend_kernel,
        out_shape=shape((CHIPS, BLOCK, HEAD), BF16),
        in_specs=[spec(SMEM)] + [spec(VMEM)] * (6 + SENDS),
        out_specs=spec(VMEM),
        compiler_params=params,
        name="attend",
    )(lengths, every_query, own, node, mask, order, turned, *peers)

    parts = lax.all_to_all(partial, ("x", "y"), 0, 0, tiled=True)
    mixed = pl.pallas_call(
        combine_kernel,
        out_shape=shape((CHIPS, BLOCK, HEAD), BF16),
        in_specs=[spec(SMEM), spec(VMEM)],
        out_specs=spec(VMEM),
        compiler_params=params,
        name="combine",
    )(path, parts)
    attention = lax.all_to_all(mixed, ("x", "y"), 0, 0, tiled=True)

    sums = pl.pallas_call(
        project_kernel,
        grid=(1,),
        out_shape=shape((16, HALF, 8, HEAD), F32),
        in_specs=[
            pl.BlockSpec((CHIPS, BLOCK, HEAD), lambda i: (0, 0, 0)),
            pl.BlockSpec((8 * HEAD, HEAD), lambda i: (0, 0)),
            pl.BlockSpec((W_ROWS, 2 * HEAD), lambda i: (0, 0)),
        ],
        out_specs=pl.BlockSpec((16, HALF, 8, HEAD), lambda i: (0, 0, 0, 0)),
        compiler_params=params,
        name="project",
    )(attention, out_weight, peers[1])
    shares = lax.all_to_all(sums, ("core", "tp"), 0, 0, tiled=True)
    projected = pl.pallas_call(
        sum_kernel,
        out_shape=shape((REQUESTS, 8, HEAD), F32),
        in_specs=[spec(VMEM)],
        out_specs=spec(VMEM),
        compiler_params=params,
        name="sum",
    )(shares)

    updated_pool, new_table = pl.pallas_call(
        write_kernel,
        out_shape=(shape(pool.shape, pool.dtype), shape(table.shape, table.dtype)),
        in_specs=[spec(SMEM)] * 4 + [spec(VMEM), spec(VMEM), spec(HBM)],
        out_specs=(spec(HBM), spec(SMEM)),
        input_output_aliases={6: 0},
        scratch_shapes=[VMEM((2 * REQUESTS, PAGE, 2 * HEAD), BF16), pltpu.SemaphoreType.DMA((2 * REQUESTS,))],
        compiler_params=params,
        name="write",
    )(table, lengths, counts, free_slot, table, attention, pool_copy)
    return projected, updated_pool, new_table


def solution(mesh):
    fine = Mesh(mesh.devices.reshape(4, 8, 2, 8), ("x", "y", "core", "tp"))
    ctx = ("x", "y", "core")
    placed = (
        P(None, ctx, "tp"),
        P(None, ctx, "tp"),
        P(ctx, None, "tp"),
        P("tp", ctx),
        P(),
        P(),
        P(),
        P(),
        P(None, ctx),
        P(None, ctx),
    )
    return jax.shard_map(
        on_device,
        mesh=fine,
        in_specs=placed,
        out_specs=(P(None, "tp", ctx), P(ctx, None, "tp"), P(None, ctx)),
        check_vma=False,
    )
```
